768 devices in a mesh: gx: 24 (over y_hi, z), gy: 8 (over y_lo, core), gz: 4 (over x).
Axes of the slice: x: 4, y: 8 (y_hi: 2, y_lo: 4; y = y_hi * 4 + y_lo), z: 12, core: 2. Of those that a mesh axis runs over, the one named last changes fastest.
Arguments:
- state: float32 [5, 192, 64, 512], P(None, 'gx', 'gy', 'gz'), may hold values from -3 to 210, as said below
- register: float32 [5, 192, 64, 512], P(None, 'gx', 'gy', 'gz'), may hold values from -0.5 to 0.5, as said below
Outputs:
- state_next: float32 [5, 192, 64, 512], P(None, 'gx', 'gy', 'gz')
- register_next: float32 [5, 192, 64, 512], P(None, 'gx', 'gy', 'gz')
- coefficients: float32 [2, 192, 64, 512], P(None, 'gx', 'gy', 'gz')
The draws below stay inside these ranges and needn't reach their ends.
Inputs may be any that keep to these rules, and one draw needn't show every extreme that they name: In every cell the density state[0] lies between 0.125 and 2 and the pressure 0.4 (state[4] - 0.5 (state[1]^2 + state[2]^2 + state[3]^2) / state[0]) is 0.5 or more, up to rounding. The density component register[0] lies within -0.06 and 0.06.
All inputs are finite; a program needn't handle non-finite values.
Results may differ from the reference program's by a relative error of at most 0.00002.
Values sent between devices are 32-bit elements; how exact they have to be, the bound alone decides.
A program may use at most 64 MiB of HBM per device.

```python
import math
import jax
import jax.numpy as jnp
from jax import lax

LEVELS = 2
NX = 192
NY = 64
NZ = 512


def wrap_gap(extent, middle):
    offsets = jnp.abs(jnp.arange(extent, dtype=jnp.int32) - middle)
    return jnp.minimum(offsets, extent - offsets).astype(jnp.float32)


def draw_state(key, part):
    key = jax.random.fold_in(key, 11)
    subkeys = jax.random.split(key, 4)
    grid_shape = (NX, NY, NZ)
    base_density = jnp.exp(jax.random.uniform(subkeys[0], grid_shape, jnp.float32, math.log(0.5), math.log(2.0)))
    velocity = jnp.clip(0.6 * jax.random.normal(subkeys[1], (3,) + grid_shape, jnp.float32), -1.5, 1.5)
    base_pressure = jnp.exp(jax.random.uniform(subkeys[2], grid_shape, jnp.float32, math.log(0.5), math.log(2.5)))
    centre = jax.random.randint(subkeys[3], (3,), 0, jnp.array([NX, NY, NZ], jnp.int32))
    radius = jnp.square(wrap_gap(NX, centre[0]))[:, None, None] + jnp.square(wrap_gap(NY, centre[1]))[None, :, None] + jnp.square(wrap_gap(NZ, centre[2]))[None, None, :]
    hotspot = jnp.exp(-radius / 4.5)
    density = base_density / (1.0 + 3.0 * hotspot)
    pressure = base_pressure * (1.0 + 31.0 * hotspot)
    energy = pressure / 0.4 + 0.5 * density * (velocity[0] * velocity[0] + velocity[1] * velocity[1] + velocity[2] * velocity[2])
    return jnp.stack([density, density * velocity[0], density * velocity[1], density * velocity[2], energy])


def draw_register(key, part):
    key = jax.random.fold_in(key, 23)
    scales = jnp.array([0.01, 0.05, 0.05, 0.05, 0.05], jnp.float32)[:, None, None, None]
    values = jnp.clip(jax.random.normal(key, (5, NX, NY, NZ), jnp.float32), -5.0, 5.0)
    return scales * values


def setup_inputs(seed: int = 0) -> dict:
    seeds = jax.random.split(jax.random.key(seed), 3)
    state = draw_state(jax.random.fold_in(seeds[2], 71), 0)
    register = draw_register(jax.random.fold_in(seeds[2], 71), 0)
    return dict(state=state, register=register)


WENO_EPS = 1e-06
CFL_NUMBER = 0.3
SECTION_DECAY = -5.0 / 9.0
SECTION_GAIN = 15.0 / 16.0

def primitives(state):
    density = state[0]
    u = state[1] / density
    v = state[2] / density
    w = state[3] / density
    pressure = 0.4 * (state[4] - 0.5 * density * (u * u + v * v + w * w))
    return jnp.stack([density, u, v, w, pressure])

def weno_face(a, b, c, d, e):
    cand_one = (2.0 * a - 7.0 * b + 11.0 * c) * (1.0 / 6.0)
    cand_two = (-b + 5.0 * c + 2.0 * d) * (1.0 / 6.0)
    cand_three = (2.0 * c + 5.0 * d - e) * (1.0 / 6.0)
    beta_one = 13.0 / 12.0 * jnp.square(a - 2.0 * b + c) + 0.25 * jnp.square(a - 4.0 * b + 3.0 * c)
    beta_two = 13.0 / 12.0 * jnp.square(b - 2.0 * c + d) + 0.25 * jnp.square(b - d)
    beta_three = 13.0 / 12.0 * jnp.square(c - 2.0 * d + e) + 0.25 * jnp.square(3.0 * c - 4.0 * d + e)
    weight_one = 0.1 / jnp.square(WENO_EPS + beta_one)
    weight_two = 0.6 / jnp.square(WENO_EPS + beta_two)
    weight_three = 0.3 / jnp.square(WENO_EPS + beta_three)
    total = weight_one * cand_one + weight_two * cand_two + weight_three * cand_three
    return total / (weight_one + weight_two + weight_three)

def floor_face(face, lower_cell, upper_cell):
    floor_value = 0.5 * jnp.minimum(lower_cell, upper_cell)
    return jnp.stack([jnp.maximum(face[0], floor_value[0]), face[1], face[2], face[3], jnp.maximum(face[4], floor_value[4])])

def state_terms(primitive, dimension):
    density, u, v, w, pressure = (primitive[0], primitive[1], primitive[2], primitive[3], primitive[4])
    normal = primitive[dimension]
    energy = pressure / 0.4 + 0.5 * density * (u * u + v * v + w * w)
    conserved = jnp.stack([density, density * u, density * v, density * w, energy])
    momentum = [density * u * normal, density * v * normal, density * w * normal]
    momentum[dimension - 1] = momentum[dimension - 1] + pressure
    fluxes = jnp.stack([density * normal] + momentum + [(energy + pressure) * normal])
    sound = jnp.sqrt(1.4 * pressure / density)
    return (conserved, fluxes, normal, sound)

def hlle_flux(left_state, right_state, dimension):
    conserved_left, flux_left, normal_left, sound_left = state_terms(left_state, dimension)
    conserved_right, flux_right, normal_right, sound_right = state_terms(right_state, dimension)
    lower = jnp.minimum(jnp.minimum(normal_left - sound_left, normal_right - sound_right), 0.0)
    upper = jnp.maximum(jnp.maximum(normal_left + sound_left, normal_right + sound_right), 0.0)
    return (upper * flux_left - lower * flux_right + upper * lower * (conserved_right - conserved_left)) / (upper - lower)

def face_change(primitive, dimension):
    shifted = [jnp.roll(primitive, 2 - index, axis=dimension) for index in range(6)]
    left_state = floor_face(weno_face(shifted[0], shifted[1], shifted[2], shifted[3], shifted[4]), shifted[2], shifted[3])
    right_state = floor_face(weno_face(shifted[5], shifted[4], shifted[3], shifted[2], shifted[1]), shifted[2], shifted[3])
    fluxes = hlle_flux(left_state, right_state, dimension)
    return fluxes - jnp.roll(fluxes, 1, axis=dimension)

def pair_up(even_part, odd_part, dimension):
    joined = jnp.stack([even_part, odd_part], axis=dimension + 1)
    new_shape = list(even_part.shape)
    new_shape[dimension] = 2 * new_shape[dimension]
    return joined.reshape(new_shape)

def lift_periodic(coarse, dimension):
    length = coarse.shape[dimension]
    even_part = lax.slice_in_dim(coarse, 0, length, 2, dimension)
    odd_part = lax.slice_in_dim(coarse, 1, length, 2, dimension)
    predicted = (9.0 * (even_part + jnp.roll(even_part, -1, axis=dimension)) - (jnp.roll(even_part, 1, axis=dimension) + jnp.roll(even_part, -2, axis=dimension))) * 0.0625
    return pair_up(even_part, odd_part - predicted, dimension)

def reference(state, register):
    primitive = primitives(state)
    speed = jnp.maximum(jnp.maximum(jnp.abs(primitive[1]), jnp.abs(primitive[2])), jnp.abs(primitive[3])) + jnp.sqrt(1.4 * primitive[4] / primitive[0])
    step_size = CFL_NUMBER / jnp.max(speed)
    change = face_change(primitive, 1)
    change = change + face_change(primitive, 2)
    change = change + face_change(primitive, 3)
    register_next = SECTION_DECAY * register + step_size * -change
    state_next = state + SECTION_GAIN * register_next
    after = primitives(state_next)
    coefficients = jnp.stack([after[4], after[0]])
    for level_index in range(LEVELS):
        stride = 2 ** level_index
        coarse = coefficients[:, ::stride, ::stride, ::stride]
        for dimension in (1, 2, 3):
            coarse = lift_periodic(coarse, dimension)
        coefficients = coefficients.at[:, ::stride, ::stride, ::stride].set(coarse)
    return (state_next, register_next, coefficients)
```

```python
import functools

import jax
import jax.numpy as jnp
from jax import lax
from jax.experimental import pallas as pl
from jax.experimental.pallas import tpu as pltpu
from jax.sharding import PartitionSpec as P

F32 = jnp.float32
CFL_NUMBER = 0.3
SECTION_DECAY = -5.0 / 9.0
SECTION_GAIN = 15.0 / 16.0
NF = 5
LX = 8
LZ = 128
SPARE = (LX + 6) * 8


def weno_pair(a, b, c, d, e):
    e1 = b - a
    e2 = c - b
    e3 = d - c
    e4 = e - d
    d0 = e2 - e1
    d1 = e3 - e2
    d2 = e4 - e3
    g0 = d0 + 2.0 * e2
    g1 = e2 + e3
    g2 = d2 - 2.0 * e3
    third = 13.0 / 3.0
    s0 = (third * d0) * d0 + g0 * g0 + 4e-6
    s1 = (third * d1) * d1 + g1 * g1 + 4e-6
    s2 = (third * d2) * d2 + g2 * g2 + 4e-6
    t0 = s0 * s0
    t1 = s1 * s1
    t2 = s2 * s2
    n0 = t1 * t2
    n1 = 6.0 * (t0 * t2)
    n2 = t0 * t1
    n0_three = 3.0 * n0
    n2_three = 3.0 * n2
    left_up = n0 * (5.0 * e2 - 2.0 * e1) + n1 * (2.0 * e3 + e2) + n2_three * (4.0 * e3 - e4)
    right_up = n2 * (5.0 * e3 - 2.0 * e4) + n1 * (2.0 * e2 + e3) + n0_three * (4.0 * e2 - e1)
    left = c + left_up / (6.0 * (n0 + n1 + n2_three))
    right = c - right_up / (6.0 * (n2 + n1 + n0_three))
    return left, right


def floored(face, lower, upper):
    return (
        jnp.maximum(face[0], 0.5 * jnp.minimum(lower[0], upper[0])),
        face[1],
        face[2],
        face[3],
        jnp.maximum(face[4], 0.5 * jnp.minimum(lower[1], upper[1])),
    )


def hlle(left, right, normal):
    def terms(s):
        rho, u, v, w, p = s
        sound = jnp.sqrt(1.4 * p / rho)
        energy = 2.5 * p + 0.5 * rho * (u * u + v * v + w * w)
        return (rho, rho * u, rho * v, rho * w, energy), s[normal], sound

    ul, nl, cl = terms(left)
    ur, nr, cr = terms(right)
    sm = jnp.minimum(jnp.minimum(nl - cl, nr - cr), 0.0)
    sp = jnp.maximum(jnp.maximum(nl + cl, nr + cr), 0.0)
    inv = 1.0 / (sp - sm)
    spi = sp * inv
    smi = sm * inv
    al = spi * (nl - sm)
    ar = smi * (sp - nr)
    pl_ = spi * left[4]
    pr_ = smi * right[4]
    flux = [al * ul[k] + ar * ur[k] for k in range(NF)]
    flux[normal] = flux[normal] + (pl_ - pr_)
    flux[4] = flux[4] + (pl_ * nl - pr_ * nr)
    return tuple(flux)


def kernel(
    sizes,
    state,
    register,
    o_state,
    o_reg,
    o_coef,
    st,
    rg,
    px,
    py,
    ez,
    ezl,
    ezh,
    ch_x,
    ch_y,
    fz,
    sn,
    rn,
    fe,
    fel,
    feh,
    g0,
    g1,
    mm,
    ml,
    mh,
    sx_hi,
    sx_lo,
    sm_hi,
    sm_lo,
    rx_lo,
    rx_hi,
    cl_lo,
    cl_hi,
    ch_lo,
    ch_hi,
    y0,
    y1,
    mx,
    my,
    mz,
    local_sem,
    halo_send,
    halo_recv,
    max_send,
    max_recv,
    lift_send,
    lift_recv,
):
    nx, ny, nz = sizes
    ix = lax.axis_index("gx")
    iy = lax.axis_index("gy")
    iz = lax.axis_index("gz")

    def at(dx=0, dy=0, dz=0):
        return {
            "gx": lax.rem(ix + (dx + nx), nx),
            "gy": lax.rem(iy + (dy + ny), ny),
            "gz": lax.rem(iz + (dz + nz), nz),
        }

    barrier = pltpu.get_barrier_semaphore()

    def greet(target):
        pl.semaphore_signal(barrier, inc=1, device_id=target, device_id_type=pl.DeviceIdType.MESH)

    load_state = pltpu.make_async_copy(state, st, local_sem.at[0])
    load_reg = pltpu.make_async_copy(register, rg, local_sem.at[1])
    load_state.start()
    load_reg.start()
    for k in range(1, nz):
        greet(at(dz=k))
    for k in range(1, ny):
        greet(at(dy=k))

    def greet_x(k, _):
        greet(at(dx=k))
        return 0

    lax.fori_loop(1, nx, greet_x, 0)
    for dx in (-1, 1):
        for dy in (-1, 1):
            greet(at(dx=dx, dy=dy))
    partners = (nx - 1) + (ny - 1) + (nz - 1) + 4

    lane = lax.broadcasted_iota(jnp.int32, (8, LZ), 1)
    row = lax.broadcasted_iota(jnp.int32, (8, LZ), 0)
    group = lane // 16
    inner = lane % 16

    load_state.wait()

    def make_primitives(x, carry):
        top, edges = carry
        rho = st[0, x]
        inv = 1.0 / rho
        u = st[1, x] * inv
        v = st[2, x] * inv
        w = st[3, x] * inv
        p = 0.4 * (st[4, x] - 0.5 * rho * (u * u + v * v + w * w))
        here = (rho, u, v, w, p)
        rows = pl.ds(pl.multiple_of((x + 3) * 8, 8), 8)
        packed = []
        for k in range(NF):
            px[k, rows, :] = here[k]
            turned = pltpu.roll(here[k], 16 * x + 3, 1)
            packed.append(jnp.where(group == x, turned, edges[k]))
        speed = jnp.maximum(jnp.maximum(jnp.abs(u), jnp.abs(v)), jnp.abs(w)) + jnp.sqrt(1.4 * p * inv)
        return jnp.maximum(top, speed), tuple(packed)

    zero = jnp.zeros((8, LZ), F32)
    top, edges = lax.fori_loop(0, LX, make_primitives, (zero, (zero,) * NF))
    for k in range(NF):
        ez[k] = edges[k]
    top = jnp.max(jnp.max(top, axis=0, keepdims=True), axis=1, keepdims=True)
    mz[0] = jnp.broadcast_to(top, (1, LZ))

    def turn(y, _):
        rows = pl.ds(pl.multiple_of((y + 3) * 8, 8), 8)
        for k in range(NF):
            py[k, rows, :] = px[k, pl.ds(24 + y, 8, stride=8), :]
        return 0

    lax.fori_loop(0, LX, turn, 0)

    pl.semaphore_wait(barrier, partners)

    def remote(src, dst, send, recv, target):
        return pltpu.make_async_remote_copy(
            src_ref=src,
            dst_ref=dst,
            send_sem=send,
            recv_sem=recv,
            device_id=target,
            device_id_type=pl.DeviceIdType.MESH,
        )

    def max_copy(slots, base, k, target):
        return remote(slots.at[0], slots.at[k], max_send.at[base + k], max_recv.at[base + k], target)

    def max_start(slots, count, base, name):
        def body(k, _):
            max_copy(slots, base, k, at(**{name: k})).start()
            return 0

        lax.fori_loop(1, count, body, 0)

    def max_wait(slots, count, base, name):
        def body(k, best):
            max_copy(slots, base, k, at(**{name: k})).wait_recv()
            return jnp.maximum(best, slots[k])

        return lax.fori_loop(1, count, body, slots[0])

    def max_sent(slots, count, base, name):
        def body(k, _):
            max_copy(slots, base, k, at(**{name: k})).wait_send()
            return 0

        lax.fori_loop(1, count, body, 0)

    low, high = pl.ds(0, 24), pl.ds(88, 24)
    first, last = pl.ds(24, 24), pl.ds(64, 24)
    halos = [
        remote(ez, ezl, halo_send.at[0], halo_recv.at[0], at(dz=1)),
        remote(ez, ezh, halo_send.at[1], halo_recv.at[1], at(dz=-1)),
        remote(py.at[:, last, :], py.at[:, low, :], halo_send.at[2], halo_recv.at[2], at(dy=1)),
        remote(py.at[:, first, :], py.at[:, high, :], halo_send.at[3], halo_recv.at[3], at(dy=-1)),
        remote(px.at[:, last, :], px.at[:, low, :], halo_send.at[4], halo_recv.at[4], at(dx=1)),
        remote(px.at[:, first, :], px.at[:, high, :], halo_send.at[5], halo_recv.at[5], at(dx=-1)),
    ]
    max_start(mz, nz, 0, "dz")
    for copy in (halos[4], halos[5], halos[2], halos[3], halos[0], halos[1]):
        copy.start()
    my[0] = max_wait(mz, nz, 0, "dz")
    max_start(my, ny, nz, "dy")

    halos[0].wait_recv()
    halos[1].wait_recv()
    for k in range(NF):
        lower = jnp.where(inner < 3, ezl[k], ez[k])
        upper = pltpu.roll(jnp.where(inner < 3, ez[k], ezh[k]), 8, 1)
        px[k, pl.ds(SPARE, 8), :] = jnp.where(inner < 8, lower, upper)

    def z_faces(x, _):
        rows = pl.ds(pl.multiple_of((x + 3 + 3 * (x // LX)) * 8, 8), 8)
        left, right, cell, nxt = [], [], [], []
        for k in range(NF):
            c = px[k, rows, :]
            outside = pltpu.roll(jnp.where(inner < 3, ezl[k], ezh[k]), lax.rem(253 - 16 * x, LZ), 1)
            a = pltpu.roll(jnp.where(lane >= LZ - 2, outside, c), 2, 1)
            b = pltpu.roll(jnp.where(lane >= LZ - 1, outside, c), 1, 1)
            d = pltpu.roll(jnp.where(lane < 1, outside, c), LZ - 1, 1)
            e = pltpu.roll(jnp.where(lane < 2, outside, c), LZ - 2, 1)
            lk, rk = weno_pair(a, b, c, d, e)
            left.append(lk)
            right.append(pltpu.roll(rk, LZ - 1, 1))
            cell.append(c)
            nxt.append(d)
        sides = (cell[0], cell[4]), (nxt[0], nxt[4])
        flux = hlle(floored(left, *sides), floored(right, *sides), 3)
        out = pl.ds(pl.multiple_of(x * 8, 8), 8)
        for k in range(NF):
            fz[k, out, :] = flux[k]
        return 0

    lax.fori_loop(0, LX + 1, z_faces, 0)
    for k in range(NF):
        ends = fz[k, pl.ds(64, 8), :]
        fz[k, pl.ds(64, 8), :] = jnp.where(inner == 11, pltpu.roll(ends, 9, 1), ends)

    mx[0] = max_wait(my, ny, nz, "dy")
    max_start(mx, nx, nz + ny, "dx")

    def sweep(padded, change, normal):
        def body(j, carry):
            before, flux_before = carry
            left, right = [], []
            lower, upper = [], []
            for k in range(NF):
                a, b, c, d, e = (
                    padded[k, pl.ds(pl.multiple_of((j + i) * 8, 8), 8), :] for i in range(5)
                )
                lk, rk = weno_pair(a, b, c, d, e)
                left.append(lk)
                right.append(rk)
                if k in (0, 4):
                    lower.append(b)
                    upper.append(c)
            sides = tuple(lower), tuple(upper)
            flux = hlle(floored(before, *sides), floored(right, *sides), normal)
            out = pl.ds(pl.multiple_of(j * 8, 8), 8)
            for k in range(NF):
                change[k, out, :] = flux[k] - flux_before[k]
            return tuple(left), flux

        one = jnp.ones((8, LZ), F32)
        lax.fori_loop(0, LX + 2, body, ((one,) * NF, (one,) * NF))

    halos[2].wait_recv()
    halos[3].wait_recv()
    sweep(py, ch_y, 2)
    halos[4].wait_recv()
    halos[5].wait_recv()
    sweep(px, ch_x, 1)

    load_reg.wait()
    fastest = max_wait(mx, nx, nz + ny, "dx")
    step = jnp.broadcast_to(CFL_NUMBER / fastest, (8, LZ))

    def update(x, edges):
        rows_x = pl.ds(pl.multiple_of((x + 2) * 8, 8), 8)
        rows_z = pl.ds(pl.multiple_of(x * 8, 8), 8)
        new = []
        for k in range(NF):
            faces = fz[k, rows_z, :]
            ends = pltpu.roll(fz[k, pl.ds(64, 8), :], 117 - 16 * x, 1)
            upper = jnp.where(lane == LZ - 1, ends, faces)
            lower = jnp.where(lane == 0, ends, pltpu.roll(faces, 1, 1))
            change = ch_x[k, rows_x, :] + ch_y[k, pl.ds(16 + x, 8, stride=8), :]
            change = change + (upper - lower)
            r = SECTION_DECAY * rg[k, x] - step * change
            s = st[k, x] + SECTION_GAIN * r
            rn[k, x] = r
            sn[k, x] = s
            new.append(s)
        rho = new[0]
        square = new[1] * new[1] + new[2] * new[2] + new[3] * new[3]
        p = 0.4 * (new[4] - 0.5 * square / rho)
        packed = []
        for f, value in enumerate((p, rho)):
            g0[f, x] = value
            packed.append(jnp.where(group == x, pltpu.roll(value, 16 * x + 4, 1), edges[f]))
        return tuple(packed)

    edges = lax.fori_loop(0, LX, update, (zero, zero))
    store_state = pltpu.make_async_copy(sn, o_state, local_sem.at[2])
    store_reg = pltpu.make_async_copy(rn, o_reg, local_sem.at[3])
    fe[0] = edges[0]
    fe[1] = edges[1]
    z_copies = [
        remote(fe, fel, lift_send.at[0], lift_recv.at[0], at(dz=1)),
        remote(fe, feh, lift_send.at[1], lift_recv.at[1], at(dz=-1)),
    ]
    for copy in z_copies:
        copy.start()
    store_state.start()
    store_reg.start()
    for copy in z_copies:
        copy.wait_recv()

    odd_lane = lane % 2 == 1
    mid_lane = lane % 4 == 2

    def lift_z(x, _):
        for f in range(2):
            c = g0[f, x]
            out = pltpu.roll(jnp.where(inner < 4, fel[f], feh[f]), lax.rem(252 - 16 * x, LZ), 1)
            up1 = pltpu.roll(jnp.where(lane < 1, out, c), LZ - 1, 1)
            up3 = pltpu.roll(jnp.where(lane < 3, out, c), LZ - 3, 1)
            down1 = pltpu.roll(c, 1, 1)
            down3 = pltpu.roll(jnp.where(lane >= LZ - 3, out, c), 3, 1)
            up2 = pltpu.roll(jnp.where(lane < 2, out, c), LZ - 2, 1)
            up6 = pltpu.roll(jnp.where(lane < 6, out, c), LZ - 6, 1)
            down2 = pltpu.roll(c, 2, 1)
            down6 = pltpu.roll(jnp.where(lane >= LZ - 6, out, c), 6, 1)
            fine = c - (9.0 * (down1 + up1) - (down3 + up3)) * 0.0625
            coarse = c - (9.0 * (down2 + up2) - (down6 + up6)) * 0.0625
            fine = jnp.where(odd_lane, fine, c)
            coarse = jnp.where(mid_lane, coarse, c)
            g0[f, x] = fine
            g1[f, x] = coarse
            merged = jnp.where(row == 1, pltpu.roll(coarse, 1, 0), jnp.where(row == 4, coarse, fine))
            mm[f, x] = merged
        return 0

    lax.fori_loop(0, LX, lift_z, 0)
    for f in range(2):
        for i, (g, x) in enumerate(((g0, 6), (g1, 4))):
            sx_hi[f, i] = g[f, x]
            sm_hi[f, i] = mm[f, x]
        for i, (g, x) in enumerate(((g0, 0), (g0, 2), (g1, 0), (g1, 4))):
            sx_lo[f, i] = g[f, x]
        for i, x in enumerate((0, 2, 4)):
            sm_lo[f, i] = mm[f, x]
    xy_copies = [
        remote(sx_hi, rx_lo, lift_send.at[2], lift_recv.at[2], at(dx=1)),
        remote(sx_lo, rx_hi, lift_send.at[3], lift_recv.at[3], at(dx=-1)),
        remote(mm, ml, lift_send.at[4], lift_recv.at[4], at(dy=1)),
        remote(mm, mh, lift_send.at[5], lift_recv.at[5], at(dy=-1)),
        remote(sm_hi, cl_lo, lift_send.at[6], lift_recv.at[6], at(dx=1, dy=1)),
        remote(sm_hi, cl_hi, lift_send.at[7], lift_recv.at[7], at(dx=1, dy=-1)),
        remote(sm_lo, ch_lo, lift_send.at[8], lift_recv.at[8], at(dx=-1, dy=1)),
        remote(sm_lo, ch_hi, lift_send.at[9], lift_recv.at[9], at(dx=-1, dy=-1)),
    ]
    for copy in xy_copies:
        copy.start()
    for copy in xy_copies:
        copy.wait_recv()

    odd_row = row % 2 == 1
    mid_row = row % 4 == 2

    def fine_y(c, lower, upper):
        up1 = pltpu.roll(jnp.where(row == 0, upper, c), 7, 0)
        up3 = pltpu.roll(jnp.where(row < 3, upper, c), 5, 0)
        down1 = pltpu.roll(c, 1, 0)
        down3 = pltpu.roll(jnp.where(row == 6, lower, c), 3, 0)
        return jnp.where(odd_row, c - (9.0 * (down1 + up1) - (down3 + up3)) * 0.0625, c)

    def coarse_y(c, lower, upper):
        up2 = jnp.where(row == 6, pltpu.roll(upper, 5, 0), pltpu.roll(c, 6, 0))
        up6 = jnp.where(row == 6, pltpu.roll(upper, 2, 0), pltpu.roll(upper, 1, 0))
        down2 = pltpu.roll(c, 2, 0)
        down6 = pltpu.roll(jnp.where(row == 4, lower, c), 6, 0)
        return jnp.where(mid_row, c - (9.0 * (down2 + up2) - (down6 + up6)) * 0.0625, c)

    for f in range(2):

        def lift_y(x, _, f=f):
            y0[f, x + 1] = fine_y(g0[f, x], ml[f, x], mh[f, x])
            return 0

        lax.fori_loop(0, LX, lift_y, 0)

        def lift_y_coarse(i, _, f=f):
            y1[f, i + 1] = coarse_y(g1[f, 2 * i], ml[f, 2 * i], mh[f, 2 * i])
            return 0

        lax.fori_loop(0, LX // 2, lift_y_coarse, 0)
        y0[f, 0] = fine_y(rx_lo[f, 0], cl_lo[f, 0], cl_hi[f, 0])
        y0[f, 9] = fine_y(rx_hi[f, 0], ch_lo[f, 0], ch_hi[f, 0])
        y0[f, 10] = fine_y(rx_hi[f, 1], ch_lo[f, 1], ch_hi[f, 1])
        y1[f, 0] = coarse_y(rx_lo[f, 1], cl_lo[f, 1], cl_hi[f, 1])
        y1[f, 5] = coarse_y(rx_hi[f, 2], ch_lo[f, 0], ch_hi[f, 0])
        y1[f, 6] = coarse_y(rx_hi[f, 3], ch_lo[f, 2], ch_hi[f, 2])

    even = jnp.logical_and(row % 2 == 0, lane % 2 == 0)
    for f in range(2):
        plane = [y0[f, i] for i in range(11)]
        coarse = [y1[f, i] for i in range(7)]
        fine = {-2: plane[0], 8: plane[9], 10: plane[10]}
        for x in range(LX):
            fine[x] = plane[x + 1]
        for x in range(1, LX, 2):
            guess = (9.0 * (fine[x - 1] + fine[x + 1]) - (fine[x - 3] + fine[x + 3])) * 0.0625
            y0[f, x] = fine[x] - guess
        far = {-4: coarse[0], 0: coarse[1], 2: coarse[2], 4: coarse[3], 6: coarse[4], 8: coarse[5], 12: coarse[6]}
        for x in range(0, LX, 2):
            value = far[x]
            if x % 4 == 2:
                value = value - (9.0 * (far[x - 2] + far[x + 2]) - (far[x - 6] + far[x + 6])) * 0.0625
            g1[f, x] = jnp.where(even, value, fine[x])
        for x in range(1, LX, 2):
            g1[f, x] = y0[f, x]
    store_coef = pltpu.make_async_copy(g1, o_coef, local_sem.at[4])
    store_coef.start()

    for copy in halos + z_copies + xy_copies:
        copy.wait_send()
    max_sent(mz, nz, 0, "dz")
    max_sent(my, ny, nz, "dy")
    max_sent(mx, nx, nz + ny, "dx")
    store_state.wait()
    store_reg.wait()
    store_coef.wait()


def solution(mesh):
    sizes = (mesh.shape["gx"], mesh.shape["gy"], mesh.shape["gz"])
    spec = P(None, "gx", "gy", "gz")
    any_space = pl.BlockSpec(memory_space=pl.ANY)

    def vmem(*shape):
        return pltpu.VMEM(shape, F32)

    plane = (8, LZ)
    total = sum(sizes)
    scratch = [
        vmem(NF, LX, *plane),
        vmem(NF, LX, *plane),
        vmem(NF, SPARE + 8, LZ),
        vmem(NF, SPARE, LZ),
        vmem(NF, *plane),
        vmem(NF, *plane),
        vmem(NF, *plane),
        vmem(NF, (LX + 2) * 8, LZ),
        vmem(NF, (LX + 2) * 8, LZ),
        vmem(NF, (LX + 1) * 8, LZ),
        vmem(NF, LX, *plane),
        vmem(NF, LX, *plane),
        vmem(2, *plane),
        vmem(2, *plane),
        vmem(2, *plane),
        vmem(2, LX, *plane),
        vmem(2, LX, *plane),
        vmem(2, LX, *plane),
        vmem(2, LX, *plane),
        vmem(2, LX, *plane),
        vmem(2, 2, *plane),
        vmem(2, 4, *plane),
        vmem(2, 2, *plane),
        vmem(2, 3, *plane),
        vmem(2, 2, *plane),
        vmem(2, 4, *plane),
        vmem(2, 2, *plane),
        vmem(2, 2, *plane),
        vmem(2, 3, *plane),
        vmem(2, 3, *plane),
        vmem(2, 11, *plane),
        vmem(2, 7, *plane),
        vmem(sizes[0], 1, LZ),
        vmem(sizes[1], 1, LZ),
        vmem(sizes[2], 1, LZ),
        pltpu.SemaphoreType.DMA((5,)),
        pltpu.SemaphoreType.DMA((6,)),
        pltpu.SemaphoreType.DMA((6,)),
        pltpu.SemaphoreType.DMA((total,)),
        pltpu.SemaphoreType.DMA((total,)),
        pltpu.SemaphoreType.DMA((10,)),
        pltpu.SemaphoreType.DMA((10,)),
    ]

    def local(state, register):
        block = jax.ShapeDtypeStruct(state.shape, F32)
        return pl.pallas_call(
            functools.partial(kernel, sizes),
            out_shape=(block, block, jax.ShapeDtypeStruct((2,) + state.shape[1:], F32)),
            in_specs=[any_space] * 2,
            out_specs=(any_space,) * 3,
            scratch_shapes=scratch,
            compiler_params=pltpu.CompilerParams(
                collective_id=0, has_side_effects=True, vmem_limit_bytes=32 * 1024 * 1024
            ),
        )(state, register)

    return jax.shard_map(local, mesh=mesh, in_specs=(spec, spec), out_specs=(spec,) * 3, check_vma=False)
```

```python
import functools

import jax
import jax.numpy as jnp
from jax import lax
from jax.experimental import pallas as pl
from jax.experimental.pallas import tpu as pltpu
from jax.sharding import PartitionSpec as P

F32 = jnp.float32
CFL_NUMBER = 0.3
SECTION_DECAY = -5.0 / 9.0
SECTION_GAIN = 15.0 / 16.0
NF = 5
LX = 8
LZ = 128
SPARE = (LX + 6) * 8


def weno_pair(a, b, c, d, e):
    e1 = b - a
    e2 = c - b
    e3 = d - c
    e4 = e - d
    d0 = e2 - e1
    d1 = e3 - e2
    d2 = e4 - e3
    g0 = d0 + 2.0 * e2
    g1 = e2 + e3
    g2 = d2 - 2.0 * e3
    third = 13.0 / 3.0
    s0 = (third * d0) * d0 + g0 * g0 + 4e-6
    s1 = (third * d1) * d1 + g1 * g1 + 4e-6
    s2 = (third * d2) * d2 + g2 * g2 + 4e-6
    t0 = s0 * s0
    t1 = s1 * s1
    t2 = s2 * s2
    n0 = t1 * t2
    n1 = 6.0 * (t0 * t2)
    n2 = t0 * t1
    n0_three = 3.0 * n0
    n2_three = 3.0 * n2
    left_up = n0 * (5.0 * e2 - 2.0 * e1) + n1 * (2.0 * e3 + e2) + n2_three * (4.0 * e3 - e4)
    right_up = n2 * (5.0 * e3 - 2.0 * e4) + n1 * (2.0 * e2 + e3) + n0_three * (4.0 * e2 - e1)
    left = c + left_up / (6.0 * (n0 + n1 + n2_three))
    right = c - right_up / (6.0 * (n2 + n1 + n0_three))
    return left, right


def floored(face, lower, upper):
    return (
        jnp.maximum(face[0], 0.5 * jnp.minimum(lower[0], upper[0])),
        face[1],
        face[2],
        face[3],
        jnp.maximum(face[4], 0.5 * jnp.minimum(lower[1], upper[1])),
    )


def hlle(left, right, normal):
    def terms(s):
        rho, u, v, w, p = s
        sound = jnp.sqrt(1.4 * p / rho)
        energy = 2.5 * p + 0.5 * rho * (u * u + v * v + w * w)
        return (rho, rho * u, rho * v, rho * w, energy), s[normal], sound

    ul, nl, cl = terms(left)
    ur, nr, cr = terms(right)
    sm = jnp.minimum(jnp.minimum(nl - cl, nr - cr), 0.0)
    sp = jnp.maximum(jnp.maximum(nl + cl, nr + cr), 0.0)
    inv = 1.0 / (sp - sm)
    spi = sp * inv
    smi = sm * inv
    al = spi * (nl - sm)
    ar = smi * (sp - nr)
    pl_ = spi * left[4]
    pr_ = smi * right[4]
    flux = [al * ul[k] + ar * ur[k] for k in range(NF)]
    flux[normal] = flux[normal] + (pl_ - pr_)
    flux[4] = flux[4] + (pl_ * nl - pr_ * nr)
    return tuple(flux)


def kernel(
    sizes,
    state,
    register,
    o_state,
    o_reg,
    o_coef,
    st,
    rg,
    px,
    py,
    ez,
    ezl,
    ezh,
    ch_x,
    ch_y,
    fz,
    sn,
    rn,
    en,
    ey,
    turned,
    around,
    sx_hi,
    sx_lo,
    rx_lo,
    rx_hi,
    sz,
    rz_lo,
    rz_hi,
    fn,
    fy,
    fc,
    coef,
    mx,
    my,
    mz,
    local_sem,
    halo_send,
    halo_recv,
    max_send,
    max_recv,
    lift_send,
    lift_recv,
):
    nx, ny, nz = sizes
    ix = lax.axis_index("gx")
    iy = lax.axis_index("gy")
    iz = lax.axis_index("gz")

    def at(dx=0, dy=0, dz=0):
        return {
            "gx": lax.rem(ix + (dx + nx), nx),
            "gy": lax.rem(iy + (dy + ny), ny),
            "gz": lax.rem(iz + (dz + nz), nz),
        }

    chips_z, half_y = nx // 2, ny // 2

    def plane_mate(k):
        return {"gx": ix, "gy": iy - iy % 2 + (iy + k // nz) % 2, "gz": (iz + k % nz) % nz}

    def column_mate(k):
        y = (ix // chips_z * half_y + iy // 2 + k) % (2 * half_y)
        return {"gx": y // half_y * chips_z + ix % chips_z, "gy": y % half_y * 2 + iy % 2, "gz": iz}

    def depth_mate(k):
        return {"gx": ix - ix % chips_z + (ix + k) % chips_z, "gy": iy, "gz": iz}

    groups = ((plane_mate, 2 * nz), (column_mate, 2 * half_y), (depth_mate, chips_z))

    barrier = pltpu.get_barrier_semaphore()

    def greet(target):
        pl.semaphore_signal(barrier, inc=1, device_id=target, device_id_type=pl.DeviceIdType.MESH)

    load_state = pltpu.make_async_copy(state, st, local_sem.at[0])
    load_reg = pltpu.make_async_copy(register, rg, local_sem.at[1])
    load_state.start()
    load_reg.start()
    for mate, count in groups:

        def greet_mate(k, _, mate=mate):
            greet(mate(k))
            return 0

        lax.fori_loop(1, count, greet_mate, 0)
    for target in (at(dx=-1), at(dx=1), at(dy=-1), at(dy=1), at(dz=-1), at(dz=1)):
        greet(target)
    partners = sum(count - 1 for _, count in groups) + 6

    lane = lax.broadcasted_iota(jnp.int32, (8, LZ), 1)
    row = lax.broadcasted_iota(jnp.int32, (8, LZ), 0)
    group = lane // 16
    inner = lane % 16

    load_state.wait()

    def make_primitives(x, top):
        rho = st[0, x]
        inv = 1.0 / rho
        u = st[1, x] * inv
        v = st[2, x] * inv
        w = st[3, x] * inv
        p = 0.4 * (st[4, x] - 0.5 * rho * (u * u + v * v + w * w))
        here = (rho, u, v, w, p)
        rows = pl.ds(pl.multiple_of((x + 3) * 8, 8), 8)
        for k in range(NF):
            px[k, rows, :] = here[k]
        speed = jnp.maximum(jnp.maximum(jnp.abs(u), jnp.abs(v)), jnp.abs(w)) + jnp.sqrt(1.4 * p * inv)
        return jnp.maximum(top, speed)

    zero = jnp.zeros((8, LZ), F32)
    top = lax.fori_loop(0, LX, make_primitives, zero)
    top = jnp.max(jnp.max(top, axis=0, keepdims=True), axis=1, keepdims=True)
    mz[0] = jnp.broadcast_to(top, (1, LZ))

    pl.semaphore_wait(barrier, partners)

    def remote(src, dst, send, recv, target):
        return pltpu.make_async_remote_copy(
            src_ref=src,
            dst_ref=dst,
            send_sem=send,
            recv_sem=recv,
            device_id=target,
            device_id_type=pl.DeviceIdType.MESH,
        )

    bases = (0, groups[0][1], groups[0][1] + groups[1][1])
    slots = (mz, my, mx)

    def max_copy(i, k):
        base = bases[i]
        return remote(slots[i].at[0], slots[i].at[k], max_send.at[base + k], max_recv.at[base + k], groups[i][0](k))

    def max_start(i):
        def body(k, _):
            max_copy(i, k).start()
            return 0

        lax.fori_loop(1, groups[i][1], body, 0)

    def max_wait(i):
        def body(k, best):
            max_copy(i, k).wait_recv()
            return jnp.maximum(best, slots[i][k])

        return lax.fori_loop(1, groups[i][1], body, slots[i][0])

    def max_sent(i):
        def body(k, _):
            max_copy(i, k).wait_send()
            return 0

        lax.fori_loop(1, groups[i][1], body, 0)

    max_start(0)

    low, high = pl.ds(0, 24), pl.ds(88, 24)
    first, last = pl.ds(24, 24), pl.ds(64, 24)
    halos = [
        remote(ez, ezl, halo_send.at[0], halo_recv.at[0], at(dz=1)),
        remote(ez, ezh, halo_send.at[1], halo_recv.at[1], at(dz=-1)),
        remote(py.at[:, last, :], py.at[:, low, :], halo_send.at[2], halo_recv.at[2], at(dy=1)),
        remote(py.at[:, first, :], py.at[:, high, :], halo_send.at[3], halo_recv.at[3], at(dy=-1)),
        remote(px.at[:, last, :], px.at[:, low, :], halo_send.at[4], halo_recv.at[4], at(dx=1)),
        remote(px.at[:, first, :], px.at[:, high, :], halo_send.at[5], halo_recv.at[5], at(dx=-1)),
    ]
    halos[4].start()
    halos[5].start()

    def turn(y, _):
        rows = pl.ds(pl.multiple_of((y + 3) * 8, 8), 8)
        for k in range(NF):
            py[k, rows, :] = px[k, pl.ds(24 + y, 8, stride=8), :]
        return 0

    lax.fori_loop(0, LX, turn, 0)
    halos[2].start()
    halos[3].start()

    def pack_edges(x, edges):
        rows = pl.ds(pl.multiple_of((x + 3) * 8, 8), 8)
        return tuple(
            jnp.where(group == x, pltpu.roll(px[k, rows, :], 16 * x + 3, 1), edges[k]) for k in range(NF)
        )

    edges = lax.fori_loop(0, LX, pack_edges, (zero,) * NF)
    for k in range(NF):
        ez[k] = edges[k]
    halos[0].start()
    halos[1].start()

    def slot(i):
        return pl.ds(8 * i if isinstance(i, int) else pl.multiple_of(i * 8, 8), 8)

    def lift_copies(v):
        def one(i, src, dst, target):
            return remote(src, dst, lift_send.at[4 * v + i], lift_recv.at[4 * v + i], target)

        to_hi, to_lo = pl.ds(0, 16), pl.ds(16, 24)
        return [
            one(0, turned.at[v, :, to_hi, :], around.at[v, :, to_hi, :], at(dy=1)),
            one(1, turned.at[v, :, to_lo, :], around.at[v, :, to_lo, :], at(dy=-1)),
            one(2, sz.at[v], rz_lo.at[v], at(dz=1)),
            one(3, sz.at[v], rz_hi.at[v], at(dz=-1)),
        ]

    lifts = [lift_copies(0), lift_copies(1)]
    for v in range(2):
        for k in range(NF):
            around[v, k, pl.ds(40, 24), :] = jnp.zeros((24, LZ), F32)

    def send_rows(v):
        for k in range(NF):
            for i, y in enumerate((4, 6, 0, 2, 4)):
                turned[v, k, pl.ds(8 * i, 8), :] = en[v, k, pl.ds(y, 8, stride=8), :]
        lifts[v][0].start()
        lifts[v][1].start()

    def send_ends(v):
        lifts[v][0].wait_recv()
        lifts[v][1].wait_recv()

        def pack_ends(x, packed):
            out = []
            for k in range(NF):
                outer = around[v, k, pl.ds(x, 8, stride=8), :]
                ey[v, k, slot(x), :] = outer
                for j, value in enumerate((en[v, k, slot(x), :], outer)):
                    out.append(jnp.where(group == x, pltpu.roll(value, 16 * x + 4, 1), packed[2 * k + j]))
            return tuple(out)

        packed = lax.fori_loop(0, LX, pack_ends, (zero,) * (2 * NF))
        for k in range(NF):
            sz[v, k, pl.ds(0, 8), :] = packed[2 * k]
            sz[v, k, pl.ds(8, 8), :] = packed[2 * k + 1]
        lifts[v][2].start()
        lifts[v][3].start()

    load_reg.wait()

    def make_base(x, _):
        for k in range(NF):
            en[0, k, slot(x), :] = st[k, x] + (SECTION_GAIN * SECTION_DECAY) * rg[k, x]
        return 0

    lax.fori_loop(0, LX, make_base, 0)
    send_rows(0)

    my[0] = max_wait(0)
    max_start(1)

    halos[0].wait_recv()
    halos[1].wait_recv()
    for k in range(NF):
        lower = jnp.where(inner < 3, ezl[k], ez[k])
        upper = pltpu.roll(jnp.where(inner < 3, ez[k], ezh[k]), 8, 1)
        px[k, pl.ds(SPARE, 8), :] = jnp.where(inner < 8, lower, upper)

    def z_faces(x, _):
        rows = pl.ds(pl.multiple_of((x + 3 + 3 * (x // LX)) * 8, 8), 8)
        left, right, cell, nxt = [], [], [], []
        for k in range(NF):
            c = px[k, rows, :]
            outside = pltpu.roll(jnp.where(inner < 3, ezl[k], ezh[k]), lax.rem(253 - 16 * x, LZ), 1)
            a = pltpu.roll(jnp.where(lane >= LZ - 2, outside, c), 2, 1)
            b = pltpu.roll(jnp.where(lane >= LZ - 1, outside, c), 1, 1)
            d = pltpu.roll(jnp.where(lane < 1, outside, c), LZ - 1, 1)
            e = pltpu.roll(jnp.where(lane < 2, outside, c), LZ - 2, 1)
            lk, rk = weno_pair(a, b, c, d, e)
            left.append(lk)
            right.append(pltpu.roll(rk, LZ - 1, 1))
            cell.append(c)
            nxt.append(d)
        sides = (cell[0], cell[4]), (nxt[0], nxt[4])
        flux = hlle(floored(left, *sides), floored(right, *sides), 3)
        out = pl.ds(pl.multiple_of(x * 8, 8), 8)
        for k in range(NF):
            fz[k, out, :] = flux[k]
        return 0

    lax.fori_loop(0, LX + 1, z_faces, 0)
    for k in range(NF):
        ends = fz[k, pl.ds(64, 8), :]
        fz[k, pl.ds(64, 8), :] = jnp.where(inner == 11, pltpu.roll(ends, 9, 1), ends)

    def sweep(padded, change, normal):
        def body(j, carry):
            before, flux_before = carry
            left, right = [], []
            lower, upper = [], []
            for k in range(NF):
                a, b, c, d, e = (
                    padded[k, pl.ds(pl.multiple_of((j + i) * 8, 8), 8), :] for i in range(5)
                )
                lk, rk = weno_pair(a, b, c, d, e)
                left.append(lk)
                right.append(rk)
                if k in (0, 4):
                    lower.append(b)
                    upper.append(c)
            sides = tuple(lower), tuple(upper)
            flux = hlle(floored(before, *sides), floored(right, *sides), normal)
            out = pl.ds(pl.multiple_of(j * 8, 8), 8)
            for k in range(NF):
                change[k, out, :] = flux[k] - flux_before[k]
            return tuple(left), flux

        one = jnp.ones((8, LZ), F32)
        lax.fori_loop(0, LX + 2, body, ((one,) * NF, (one,) * NF))

    halos[2].wait_recv()
    halos[3].wait_recv()
    sweep(py, ch_y, 2)
    send_ends(0)
    mx[0] = max_wait(1)
    max_start(2)
    halos[4].wait_recv()
    halos[5].wait_recv()
    sweep(px, ch_x, 1)

    def make_rate(x, _):
        rows_x = slot(x + 2)
        rows_z = slot(x)
        for k in range(NF):
            faces = fz[k, rows_z, :]
            ends = pltpu.roll(fz[k, pl.ds(64, 8), :], 117 - 16 * x, 1)
            upper = jnp.where(lane == LZ - 1, ends, faces)
            lower = jnp.where(lane == 0, ends, pltpu.roll(faces, 1, 1))
            change = ch_x[k, rows_x, :] + ch_y[k, pl.ds(16 + x, 8, stride=8), :]
            en[1, k, rows_z, :] = -(change + (upper - lower))
        return 0

    lax.fori_loop(0, LX, make_rate, 0)
    send_rows(1)
    send_ends(1)
    for v in range(2):
        lifts[v][2].wait_recv()
        lifts[v][3].wait_recv()

    fastest = max_wait(2)
    step = jnp.broadcast_to(CFL_NUMBER / fastest, (8, LZ))
    gain = SECTION_GAIN * step

    def pressure(new):
        square = new[1] * new[1] + new[2] * new[2] + new[3] * new[3]
        return 0.4 * (new[4] - 0.5 * square / new[0])

    from_low = inner < 4
    for j in range(2):
        rows = pl.ds(8 * j, 8)
        new = []
        for k in range(NF):
            base = jnp.where(from_low, rz_lo[0, k, rows, :], rz_hi[0, k, rows, :])
            rate = jnp.where(from_low, rz_lo[1, k, rows, :], rz_hi[1, k, rows, :])
            new.append(base + gain * rate)
        fc[0, rows, :] = pressure(new)
        fc[1, rows, :] = new[0]

    def after(ref, x):
        new = [ref[0, k, slot(x), :] + gain * ref[1, k, slot(x), :] for k in range(NF)]
        return pressure(new), new[0]

    odd_lane = lane % 2 == 1
    mid_lane = lane % 4 == 2
    odd_row = row % 2 == 1
    mid_row = row % 4 == 2

    def predicted(down1, up1, down3, up3):
        return (9.0 * (down1 + up1) - (down3 + up3)) * 0.0625

    def fine_z(c, ends):
        up1 = pltpu.roll(jnp.where(lane < 1, ends, c), LZ - 1, 1)
        up3 = pltpu.roll(jnp.where(lane < 3, ends, c), LZ - 3, 1)
        down1 = pltpu.roll(c, 1, 1)
        down3 = pltpu.roll(jnp.where(lane >= LZ - 3, ends, c), 3, 1)
        return jnp.where(odd_lane, c - predicted(down1, up1, down3, up3), c)

    def coarse_z(c, ends):
        up2 = pltpu.roll(jnp.where(lane < 2, ends, c), LZ - 2, 1)
        up6 = pltpu.roll(jnp.where(lane < 6, ends, c), LZ - 6, 1)
        down2 = pltpu.roll(c, 2, 1)
        down6 = pltpu.roll(jnp.where(lane >= LZ - 6, ends, c), 6, 1)
        return jnp.where(mid_lane, c - predicted(down2, up2, down6, up6), c)

    def fine_y(c, outer):
        down1 = pltpu.roll(c, 1, 0)
        down3 = jnp.where(row == 1, outer, pltpu.roll(c, 3, 0))
        up1 = jnp.where(row == 7, pltpu.roll(outer, 5, 0), pltpu.roll(c, 7, 0))
        up3 = jnp.where(row == 7, pltpu.roll(outer, 4, 0), pltpu.roll(c, 5, 0))
        up3 = jnp.where(row == 5, pltpu.roll(outer, 3, 0), up3)
        return jnp.where(odd_row, c - predicted(down1, up1, down3, up3), c)

    def coarse_y(c, outer):
        down2 = pltpu.roll(c, 2, 0)
        further = pltpu.roll(c, 6, 0)
        beyond = pltpu.roll(outer, 2, 0)
        up2 = jnp.where(row == 6, pltpu.roll(outer, 4, 0), further)
        down6 = jnp.where(row == 2, beyond, further)
        up6 = jnp.where(row == 2, outer, beyond)
        return jnp.where(mid_row, c - predicted(down2, up2, down6, up6), c)

    def lift_zy(x, both):
        shift = lax.rem(252 - 16 * x, LZ)
        cells, outer = after(en, x), after(ey, x)
        for f in range(2):
            ends = pltpu.roll(fc[f, pl.ds(0, 8), :], shift, 1)
            ends_outer = pltpu.roll(fc[f, pl.ds(8, 8), :], shift, 1)
            fn[f, slot(x), :] = fine_y(fine_z(cells[f], ends), fine_z(outer[f], ends_outer))
            if both:
                fy[f, slot(x), :] = coarse_y(coarse_z(cells[f], ends), coarse_z(outer[f], ends_outer))

    def lift_even(i, _):
        lift_zy(2 * i, True)
        return 0

    lax.fori_loop(0, LX // 2, lift_even, 0)

    for f in range(2):
        sx_hi[f, slot(0), :] = fn[f, slot(6), :]
        sx_hi[f, slot(1), :] = fy[f, slot(4), :]
        sx_lo[f, slot(0), :] = fn[f, slot(0), :]
        sx_lo[f, slot(1), :] = fn[f, slot(2), :]
        sx_lo[f, slot(2), :] = jnp.where(odd_row, pltpu.roll(fy[f, slot(4), :], 1, 0), fy[f, slot(0), :])
    x_copies = [
        remote(sx_hi, rx_lo, lift_send.at[8], lift_recv.at[8], at(dx=1)),
        remote(sx_lo, rx_hi, lift_send.at[9], lift_recv.at[9], at(dx=-1)),
    ]
    for copy in x_copies:
        copy.start()

    def update(x, _):
        for k in range(NF):
            r = SECTION_DECAY * rg[k, x] + step * en[1, k, slot(x), :]
            rn[k, x] = r
            sn[k, x] = st[k, x] + SECTION_GAIN * r
        return 0

    lax.fori_loop(0, LX, update, 0)
    store_state = pltpu.make_async_copy(sn, o_state, local_sem.at[2])
    store_reg = pltpu.make_async_copy(rn, o_reg, local_sem.at[3])
    store_state.start()
    store_reg.start()

    def lift_odd(i, _):
        lift_zy(2 * i + 1, False)
        return 0

    lax.fori_loop(0, LX // 2, lift_odd, 0)

    for copy in x_copies:
        copy.wait_recv()
    even = jnp.logical_and(row % 2 == 0, lane % 2 == 0)
    for f in range(2):
        fine = {x: fn[f, slot(x), :] for x in range(LX)}
        fine[-2], fine[8], fine[10] = rx_lo[f, slot(0), :], rx_hi[f, slot(0), :], rx_hi[f, slot(1), :]
        coarse = {x: fy[f, slot(x), :] for x in (0, 2, 4, 6)}
        mixed = rx_hi[f, slot(2), :]
        coarse[-4], coarse[8], coarse[12] = rx_lo[f, slot(1), :], mixed, pltpu.roll(mixed, 7, 0)
        for x in range(LX):
            if x % 2 == 1:
                coef[f, x] = fine[x] - predicted(fine[x - 1], fine[x + 1], fine[x - 3], fine[x + 3])
                continue
            value = coarse[x]
            if x % 4 == 2:
                value = value - predicted(coarse[x - 2], coarse[x + 2], coarse[x - 6], coarse[x + 6])
            coef[f, x] = jnp.where(even, value, fine[x])
    store_coef = pltpu.make_async_copy(coef, o_coef, local_sem.at[4])
    store_coef.start()

    for copy in halos + lifts[0] + lifts[1] + x_copies:
        copy.wait_send()
    for i in range(3):
        max_sent(i)
    store_state.wait()
    store_reg.wait()
    store_coef.wait()


def solution(mesh):
    sizes = (mesh.shape["gx"], mesh.shape["gy"], mesh.shape["gz"])
    spec = P(None, "gx", "gy", "gz")
    any_space = pl.BlockSpec(memory_space=pl.ANY)

    def vmem(*shape):
        return pltpu.VMEM(shape, F32)

    plane = (8, LZ)
    total = sizes[0] // 2 + sizes[1] + 2 * sizes[2]
    scratch = [
        vmem(NF, LX, *plane),
        vmem(NF, LX, *plane),
        vmem(NF, SPARE + 8, LZ),
        vmem(NF, SPARE, LZ),
        vmem(NF, *plane),
        vmem(NF, *plane),
        vmem(NF, *plane),
        vmem(NF, (LX + 2) * 8, LZ),
        vmem(NF, (LX + 2) * 8, LZ),
        vmem(NF, (LX + 1) * 8, LZ),
        vmem(NF, LX, *plane),
        vmem(NF, LX, *plane),
        vmem(2, NF, 64, LZ),
        vmem(2, NF, 64, LZ),
        vmem(2, NF, 40, LZ),
        vmem(2, NF, 64, LZ),
        vmem(2, 16, LZ),
        vmem(2, 24, LZ),
        vmem(2, 16, LZ),
        vmem(2, 24, LZ),
        vmem(2, NF, 16, LZ),
        vmem(2, NF, 16, LZ),
        vmem(2, NF, 16, LZ),
        vmem(2, 64, LZ),
        vmem(2, 64, LZ),
        vmem(2, 16, LZ),
        vmem(2, LX, *plane),
        vmem(sizes[0] // 2, 1, LZ),
        vmem(sizes[1], 1, LZ),
        vmem(2 * sizes[2], 1, LZ),
        pltpu.SemaphoreType.DMA((5,)),
        pltpu.SemaphoreType.DMA((6,)),
        pltpu.SemaphoreType.DMA((6,)),
        pltpu.SemaphoreType.DMA((total,)),
        pltpu.SemaphoreType.DMA((total,)),
        pltpu.SemaphoreType.DMA((10,)),
        pltpu.SemaphoreType.DMA((10,)),
    ]

    def local(state, register):
        block = jax.ShapeDtypeStruct(state.shape, F32)
        return pl.pallas_call(
            functools.partial(kernel, sizes),
            out_shape=(block, block, jax.ShapeDtypeStruct((2,) + state.shape[1:], F32)),
            in_specs=[any_space] * 2,
            out_specs=(any_space,) * 3,
            scratch_shapes=scratch,
            compiler_params=pltpu.CompilerParams(collective_id=0, has_side_effects=True),
        )(state, register)

    return jax.shard_map(local, mesh=mesh, in_specs=(spec, spec), out_specs=(spec,) * 3, check_vma=False)
```

```python
import functools

import jax
import jax.numpy as jnp
from jax import lax
from jax.experimental import pallas as pl
from jax.experimental.pallas import tpu as pltpu
from jax.sharding import PartitionSpec as P

F32 = jnp.float32
CFL_NUMBER = 0.3
SECTION_DECAY = -5.0 / 9.0
SECTION_GAIN = 15.0 / 16.0
NF = 5
LX = 8
LZ = 128
SPARE = (LX + 6) * 8


def weno_pair(a, b, c, d, e):
    e1 = b - a
    e2 = c - b
    e3 = d - c
    e4 = e - d
    d0 = e2 - e1
    d1 = e3 - e2
    d2 = e4 - e3
    g0 = d0 + 2.0 * e2
    g1 = e2 + e3
    g2 = d2 - 2.0 * e3
    third = 13.0 / 3.0
    s0 = (third * d0) * d0 + g0 * g0 + 4e-6
    s1 = (third * d1) * d1 + g1 * g1 + 4e-6
    s2 = (third * d2) * d2 + g2 * g2 + 4e-6
    t0 = s0 * s0
    t1 = s1 * s1
    t2 = s2 * s2
    n0 = t1 * t2
    n1 = 6.0 * (t0 * t2)
    n2 = t0 * t1
    n0_three = 3.0 * n0
    n2_three = 3.0 * n2
    left_up = n0 * (5.0 * e2 - 2.0 * e1) + n1 * (2.0 * e3 + e2) + n2_three * (4.0 * e3 - e4)
    right_up = n2 * (5.0 * e3 - 2.0 * e4) + n1 * (2.0 * e2 + e3) + n0_three * (4.0 * e2 - e1)
    left = c + left_up / (6.0 * (n0 + n1 + n2_three))
    right = c - right_up / (6.0 * (n2 + n1 + n0_three))
    return left, right


def floored(face, lower, upper):
    return (
        jnp.maximum(face[0], 0.5 * jnp.minimum(lower[0], upper[0])),
        face[1],
        face[2],
        face[3],
        jnp.maximum(face[4], 0.5 * jnp.minimum(lower[1], upper[1])),
    )


def hlle(left, right, normal):
    def terms(s):
        rho, u, v, w, p = s
        sound = jnp.sqrt(1.4 * p / rho)
        energy = 2.5 * p + 0.5 * rho * (u * u + v * v + w * w)
        return (rho, rho * u, rho * v, rho * w, energy), s[normal], sound

    ul, nl, cl = terms(left)
    ur, nr, cr = terms(right)
    sm = jnp.minimum(jnp.minimum(nl - cl, nr - cr), 0.0)
    sp = jnp.maximum(jnp.maximum(nl + cl, nr + cr), 0.0)
    inv = 1.0 / (sp - sm)
    spi = sp * inv
    smi = sm * inv
    al = spi * (nl - sm)
    ar = smi * (sp - nr)
    pl_ = spi * left[4]
    pr_ = smi * right[4]
    flux = [al * ul[k] + ar * ur[k] for k in range(NF)]
    flux[normal] = flux[normal] + (pl_ - pr_)
    flux[4] = flux[4] + (pl_ * nl - pr_ * nr)
    return tuple(flux)


def kernel(
    sizes,
    state,
    register,
    o_state,
    o_reg,
    o_coef,
    st,
    rg,
    px,
    py,
    ez,
    ezl,
    ezh,
    ch_y,
    fz,
    sn,
    rn,
    base,
    rate,
    ends,
    turned,
    around,
    sx_hi,
    sx_lo,
    rx_lo,
    rx_hi,
    sz,
    rz,
    fn,
    fy,
    fc,
    coef,
    mx,
    my,
    mz,
    local_sem,
    halo_send,
    halo_recv,
    max_send,
    max_recv,
    lift_send,
    lift_recv,
):
    nx, ny, nz = sizes
    ix = lax.axis_index("gx")
    iy = lax.axis_index("gy")
    iz = lax.axis_index("gz")

    def turned_by(i, k, n):
        k = k % n
        return i if k == 0 else jnp.where(i >= n - k, i - (n - k), i + k)

    def at(dx=0, dy=0, dz=0):
        return {"gx": turned_by(ix, dx, nx), "gy": turned_by(iy, dy, ny), "gz": turned_by(iz, dz, nz)}

    chips_z, half_y = nx // 2, ny // 2
    upper_half = jnp.where(ix >= chips_z, 1, 0)
    chip_z = ix - upper_half * chips_z
    core = lax.rem(iy, 2)
    chip_y = upper_half * half_y + lax.div(iy, 2)

    def plane_mate(k):
        return {"gx": ix, "gy": iy if k < nz else iy + 1 - 2 * core, "gz": turned_by(iz, k, nz)}

    def column_mate(k):
        y = turned_by(chip_y, k, 2 * half_y)
        half = jnp.where(y >= half_y, 1, 0)
        return {"gx": half * chips_z + chip_z, "gy": (y - half * half_y) * 2 + core, "gz": iz}

    def depth_mate(k):
        return {"gx": upper_half * chips_z + turned_by(chip_z, k, chips_z), "gy": iy, "gz": iz}

    groups = ((plane_mate, 2 * nz), (column_mate, 2 * half_y), (depth_mate, chips_z))

    def far_first(count):
        return sorted(range(1, count), key=lambda k: -min(k, count - k))

    orders = (sorted(range(1, 2 * nz), key=lambda k: -min(k % nz, nz - k % nz)), far_first(2 * half_y), far_first(chips_z))

    barrier = pltpu.get_barrier_semaphore()

    def greet(target):
        pl.semaphore_signal(barrier, inc=1, device_id=target, device_id_type=pl.DeviceIdType.MESH)

    load_state = pltpu.make_async_copy(state, st, local_sem.at[0])
    load_reg = pltpu.make_async_copy(register, rg, local_sem.at[1])
    load_state.start()
    load_reg.start()
    for (mate, _), order in zip(groups, orders):
        for k in order:
            greet(mate(k))
    for target in (at(dx=-1), at(dx=1)):
        greet(target)
    for dy in (-1, 0, 1):
        for dz in (-1, 0, 1):
            if (dy, dz) != (0, 0):
                greet(at(dy=dy, dz=dz))
    partners = sum(count - 1 for _, count in groups) + 10

    lane = lax.broadcasted_iota(jnp.int32, (8, LZ), 1)
    row = lax.broadcasted_iota(jnp.int32, (8, LZ), 0)
    group = lane // 16
    inner = lane % 16

    load_state.wait()

    def make_primitives(x, top):
        rho = st[0, x]
        inv = 1.0 / rho
        u = st[1, x] * inv
        v = st[2, x] * inv
        w = st[3, x] * inv
        p = 0.4 * (st[4, x] - 0.5 * rho * (u * u + v * v + w * w))
        here = (rho, u, v, w, p)
        rows = pl.ds(pl.multiple_of((x + 3) * 8, 8), 8)
        for k in range(NF):
            px[k, rows, :] = here[k]
        speed = jnp.maximum(jnp.maximum(jnp.abs(u), jnp.abs(v)), jnp.abs(w)) + jnp.sqrt(1.4 * p * inv)
        return jnp.maximum(top, speed)

    zero = jnp.zeros((8, LZ), F32)
    top = lax.fori_loop(0, LX, make_primitives, zero)
    top = jnp.max(jnp.max(top, axis=0, keepdims=True), axis=1, keepdims=True)
    mz[0] = jnp.broadcast_to(top, (1, LZ))

    pl.semaphore_wait(barrier, partners)

    def remote(src, dst, send, recv, target):
        return pltpu.make_async_remote_copy(
            src_ref=src,
            dst_ref=dst,
            send_sem=send,
            recv_sem=recv,
            device_id=target,
            device_id_type=pl.DeviceIdType.MESH,
        )

    bases = (0, groups[0][1], groups[0][1] + groups[1][1])
    slots = (mz, my, mx)

    def max_copy(i, k):
        sem = bases[i] + k
        return remote(slots[i].at[0], slots[i].at[k], max_send.at[sem], max_recv.at[sem], groups[i][0](k))

    def max_start(i):
        for k in orders[i]:
            max_copy(i, k).start()

    def max_wait(i):
        best = slots[i][0]
        for k in reversed(orders[i]):
            max_copy(i, k).wait_recv()
            best = jnp.maximum(best, slots[i][k])
        return best

    def max_sent(i):
        for k in orders[i]:
            max_copy(i, k).wait_send()

    max_start(0)

    low, high = pl.ds(0, 24), pl.ds(88, 24)
    first, last = pl.ds(24, 24), pl.ds(64, 24)
    halos = [
        remote(ez, ezl, halo_send.at[0], halo_recv.at[0], at(dz=1)),
        remote(ez, ezh, halo_send.at[1], halo_recv.at[1], at(dz=-1)),
        remote(py.at[:, last, :], py.at[:, low, :], halo_send.at[2], halo_recv.at[2], at(dy=1)),
        remote(py.at[:, first, :], py.at[:, high, :], halo_send.at[3], halo_recv.at[3], at(dy=-1)),
        remote(px.at[:, last, :], px.at[:, low, :], halo_send.at[4], halo_recv.at[4], at(dx=1)),
        remote(px.at[:, first, :], px.at[:, high, :], halo_send.at[5], halo_recv.at[5], at(dx=-1)),
    ]
    halos[4].start()
    halos[5].start()

    def turn(y, _):
        rows = pl.ds(pl.multiple_of((y + 3) * 8, 8), 8)
        for k in range(NF):
            py[k, rows, :] = px[k, pl.ds(24 + y, 8, stride=8), :]
        return 0

    lax.fori_loop(0, LX, turn, 0)
    halos[2].start()
    halos[3].start()

    def pack_edges(x, edges):
        rows = pl.ds(pl.multiple_of((x + 3) * 8, 8), 8)
        return tuple(
            jnp.where(group == x, pltpu.roll(px[k, rows, :], 16 * x + 3, 1), edges[k]) for k in range(NF)
        )

    edges = lax.fori_loop(0, LX, pack_edges, (zero,) * NF)
    for k in range(NF):
        ez[k] = edges[k]
    halos[0].start()
    halos[1].start()

    def slot(i):
        return pl.ds(8 * i if isinstance(i, int) else pl.multiple_of(i * 8, 8), 8)

    def plane(v, k, x):
        if v == 0:
            return base[k, slot(x), :]
        return rate[k, slot(x + 2), :]

    def lift_copies(v):
        def one(i, src, dst, target):
            return remote(src, dst, lift_send.at[8 * v + i], lift_recv.at[8 * v + i], target)

        to_hi, to_lo = pl.ds(0, 16), pl.ds(16, 24)
        copies = [
            one(0, turned.at[v, :, to_hi, :], around.at[v, :, to_hi, :], at(dy=1)),
            one(1, turned.at[v, :, to_lo, :], around.at[v, :, to_lo, :], at(dy=-1)),
        ]
        for i, (dy, dz) in enumerate(((1, 1), (1, -1), (-1, 1), (-1, -1), (0, 1), (0, -1))):
            copies.append(one(2 + i, sz.at[v], rz.at[v, i], at(dy=dy, dz=dz)))
        return copies

    lifts = [lift_copies(0), lift_copies(1)]
    for v in range(2):
        for k in range(NF):
            around[v, k, pl.ds(40, 24), :] = jnp.zeros((24, LZ), F32)

    def send_lift(v):
        source, first_row = ((base, 0), (rate, 16))[v]
        for k in range(NF):
            for i, y in enumerate((4, 6, 0, 2, 4)):
                turned[v, k, pl.ds(8 * i, 8), :] = source[k, pl.ds(first_row + y, 8, stride=8), :]
        lifts[v][0].start()
        lifts[v][1].start()

        def pack_ends(x, packed):
            return tuple(
                jnp.where(group == x, pltpu.roll(plane(v, k, x), 16 * x + 4, 1), packed[k]) for k in range(NF)
            )

        packed = lax.fori_loop(0, LX, pack_ends, (zero,) * NF)
        for k in range(NF):
            sz[v, k] = packed[k]
        for copy in lifts[v][2:]:
            copy.start()

    from_low = inner < 4

    def receive_lift(v):
        for copy in lifts[v]:
            copy.wait_recv()
        for k in range(NF):
            below = jnp.where(from_low, rz[v, 0, k], rz[v, 1, k])
            above = jnp.where(from_low, rz[v, 2, k], rz[v, 3, k])
            outer = jnp.where(row == 0, pltpu.roll(below, 4, 0), pltpu.roll(below, 3, 0))
            outer = jnp.where(row == 2, pltpu.roll(above, 2, 0), outer)
            outer = jnp.where(row == 3, pltpu.roll(above, 1, 0), outer)
            ends[v, k, pl.ds(0, 8), :] = jnp.where(from_low, rz[v, 4, k], rz[v, 5, k])
            ends[v, k, pl.ds(8, 8), :] = jnp.where(row == 4, above, outer)

    load_reg.wait()

    def make_base(x, _):
        for k in range(NF):
            base[k, slot(x), :] = st[k, x] + (SECTION_GAIN * SECTION_DECAY) * rg[k, x]
        return 0

    lax.fori_loop(0, LX, make_base, 0)
    send_lift(0)

    my[0] = max_wait(0)
    max_start(1)

    halos[0].wait_recv()
    halos[1].wait_recv()
    for k in range(NF):
        lower = jnp.where(inner < 3, ezl[k], ez[k])
        upper = pltpu.roll(jnp.where(inner < 3, ez[k], ezh[k]), 8, 1)
        px[k, pl.ds(SPARE, 8), :] = jnp.where(inner < 8, lower, upper)

    def z_faces(x, _):
        rows = pl.ds(pl.multiple_of((x + 3 + 3 * (x // LX)) * 8, 8), 8)
        left, right, cell, nxt = [], [], [], []
        for k in range(NF):
            c = px[k, rows, :]
            outside = pltpu.roll(jnp.where(inner < 3, ezl[k], ezh[k]), lax.rem(253 - 16 * x, LZ), 1)
            a = pltpu.roll(jnp.where(lane >= LZ - 2, outside, c), 2, 1)
            b = pltpu.roll(jnp.where(lane >= LZ - 1, outside, c), 1, 1)
            d = pltpu.roll(jnp.where(lane < 1, outside, c), LZ - 1, 1)
            e = pltpu.roll(jnp.where(lane < 2, outside, c), LZ - 2, 1)
            lk, rk = weno_pair(a, b, c, d, e)
            left.append(lk)
            right.append(pltpu.roll(rk, LZ - 1, 1))
            cell.append(c)
            nxt.append(d)
        sides = (cell[0], cell[4]), (nxt[0], nxt[4])
        flux = hlle(floored(left, *sides), floored(right, *sides), 3)
        out = pl.ds(pl.multiple_of(x * 8, 8), 8)
        for k in range(NF):
            fz[k, out, :] = flux[k]
        return 0

    lax.fori_loop(0, LX + 1, z_faces, 0)
    for k in range(NF):
        tail = fz[k, pl.ds(64, 8), :]
        fz[k, pl.ds(64, 8), :] = jnp.where(inner == 11, pltpu.roll(tail, 9, 1), tail)

    def sweep(padded, change, normal, subtract):
        def body(j, carry):
            before, flux_before = carry
            left, right = [], []
            lower, upper = [], []
            for k in range(NF):
                a, b, c, d, e = (
                    padded[k, pl.ds(pl.multiple_of((j + i) * 8, 8), 8), :] for i in range(5)
                )
                lk, rk = weno_pair(a, b, c, d, e)
                left.append(lk)
                right.append(rk)
                if k in (0, 4):
                    lower.append(b)
                    upper.append(c)
            sides = tuple(lower), tuple(upper)
            flux = hlle(floored(before, *sides), floored(right, *sides), normal)
            out = pl.ds(pl.multiple_of(j * 8, 8), 8)
            for k in range(NF):
                difference = flux[k] - flux_before[k]
                change[k, out, :] = change[k, out, :] - difference if subtract else difference
            return tuple(left), flux

        one = jnp.ones((8, LZ), F32)
        lax.fori_loop(0, LX + 2, body, ((one,) * NF, (one,) * NF))

    halos[2].wait_recv()
    halos[3].wait_recv()
    sweep(py, ch_y, 2, False)
    mx[0] = max_wait(1)
    max_start(2)

    def make_rate(x, _):
        for k in range(NF):
            faces = fz[k, slot(x), :]
            tips = pltpu.roll(fz[k, pl.ds(64, 8), :], 117 - 16 * x, 1)
            upper = jnp.where(lane == LZ - 1, tips, faces)
            lower = jnp.where(lane == 0, tips, pltpu.roll(faces, 1, 1))
            rate[k, slot(x + 2), :] = (lower - upper) - ch_y[k, pl.ds(16 + x, 8, stride=8), :]
        return 0

    lax.fori_loop(0, LX, make_rate, 0)
    for k in range(NF):
        rate[k, pl.ds(0, 16), :] = jnp.zeros((16, LZ), F32)
    halos[4].wait_recv()
    halos[5].wait_recv()
    sweep(px, rate, 1, True)
    send_lift(1)
    receive_lift(0)
    receive_lift(1)

    fastest = max_wait(2)
    step = jnp.broadcast_to(CFL_NUMBER / fastest, (8, LZ))
    gain = SECTION_GAIN * step

    def pressure(new):
        square = new[1] * new[1] + new[2] * new[2] + new[3] * new[3]
        return 0.4 * (new[4] - 0.5 * square / new[0])

    for j in range(2):
        new = [ends[0, k, slot(j), :] + gain * ends[1, k, slot(j), :] for k in range(NF)]
        fc[0, slot(j), :] = pressure(new)
        fc[1, slot(j), :] = new[0]

    def after(x):
        new = [plane(0, k, x) + gain * plane(1, k, x) for k in range(NF)]
        return pressure(new), new[0]

    def after_around(x):
        rows = pl.ds(x, 8, stride=8)
        new = [around[0, k, rows, :] + gain * around[1, k, rows, :] for k in range(NF)]
        return pressure(new), new[0]

    odd_lane = lane % 2 == 1
    mid_lane = lane % 4 == 2
    odd_row = row % 2 == 1
    mid_row = row % 4 == 2

    def predicted(down1, up1, down3, up3):
        return (9.0 * (down1 + up1) - (down3 + up3)) * 0.0625

    def fine_z(c, ends):
        up1 = pltpu.roll(jnp.where(lane < 1, ends, c), LZ - 1, 1)
        up3 = pltpu.roll(jnp.where(lane < 3, ends, c), LZ - 3, 1)
        down1 = pltpu.roll(c, 1, 1)
        down3 = pltpu.roll(jnp.where(lane >= LZ - 3, ends, c), 3, 1)
        return jnp.where(odd_lane, c - predicted(down1, up1, down3, up3), c)

    def coarse_z(c, ends):
        up2 = pltpu.roll(jnp.where(lane < 2, ends, c), LZ - 2, 1)
        up6 = pltpu.roll(jnp.where(lane < 6, ends, c), LZ - 6, 1)
        down2 = pltpu.roll(c, 2, 1)
        down6 = pltpu.roll(jnp.where(lane >= LZ - 6, ends, c), 6, 1)
        return jnp.where(mid_lane, c - predicted(down2, up2, down6, up6), c)

    def fine_y(c, outer):
        down1 = pltpu.roll(c, 1, 0)
        down3 = jnp.where(row == 1, outer, pltpu.roll(c, 3, 0))
        up1 = jnp.where(row == 7, pltpu.roll(outer, 5, 0), pltpu.roll(c, 7, 0))
        up3 = jnp.where(row == 7, pltpu.roll(outer, 4, 0), pltpu.roll(c, 5, 0))
        up3 = jnp.where(row == 5, pltpu.roll(outer, 3, 0), up3)
        return jnp.where(odd_row, c - predicted(down1, up1, down3, up3), c)

    def coarse_y(c, outer):
        down2 = pltpu.roll(c, 2, 0)
        further = pltpu.roll(c, 6, 0)
        beyond = pltpu.roll(outer, 2, 0)
        up2 = jnp.where(row == 6, pltpu.roll(outer, 4, 0), further)
        down6 = jnp.where(row == 2, beyond, further)
        up6 = jnp.where(row == 2, outer, beyond)
        return jnp.where(mid_row, c - predicted(down2, up2, down6, up6), c)

    def lift_zy(x, both):
        shift = lax.rem(252 - 16 * x, LZ)
        cells, outer = after(x), after_around(x)
        for f in range(2):
            tips = pltpu.roll(fc[f, pl.ds(0, 8), :], shift, 1)
            tips_outer = pltpu.roll(fc[f, pl.ds(8, 8), :], shift, 1)
            fn[f, slot(x), :] = fine_y(fine_z(cells[f], tips), fine_z(outer[f], tips_outer))
            if both:
                fy[f, slot(x), :] = coarse_y(coarse_z(cells[f], tips), coarse_z(outer[f], tips_outer))

    def lift_even(i, _):
        lift_zy(2 * i, True)
        return 0

    lax.fori_loop(0, LX // 2, lift_even, 0)

    for f in range(2):
        sx_hi[f, slot(0), :] = fn[f, slot(6), :]
        sx_hi[f, slot(1), :] = fy[f, slot(4), :]
        sx_lo[f, slot(0), :] = fn[f, slot(0), :]
        sx_lo[f, slot(1), :] = fn[f, slot(2), :]
        sx_lo[f, slot(2), :] = jnp.where(odd_row, pltpu.roll(fy[f, slot(4), :], 1, 0), fy[f, slot(0), :])
    x_copies = [
        remote(sx_hi, rx_lo, lift_send.at[16], lift_recv.at[16], at(dx=1)),
        remote(sx_lo, rx_hi, lift_send.at[17], lift_recv.at[17], at(dx=-1)),
    ]
    for copy in x_copies:
        copy.start()

    def update(x, _):
        for k in range(NF):
            r = SECTION_DECAY * rg[k, x] + step * plane(1, k, x)
            rn[k, x] = r
            sn[k, x] = st[k, x] + SECTION_GAIN * r
        return 0

    lax.fori_loop(0, LX, update, 0)
    store_state = pltpu.make_async_copy(sn, o_state, local_sem.at[2])
    store_reg = pltpu.make_async_copy(rn, o_reg, local_sem.at[3])
    store_state.start()
    store_reg.start()

    def lift_odd(i, _):
        lift_zy(2 * i + 1, False)
        return 0

    lax.fori_loop(0, LX // 2, lift_odd, 0)

    for copy in x_copies:
        copy.wait_recv()
    even = jnp.logical_and(row % 2 == 0, lane % 2 == 0)
    for f in range(2):
        fine = {x: fn[f, slot(x), :] for x in range(LX)}
        fine[-2], fine[8], fine[10] = rx_lo[f, slot(0), :], rx_hi[f, slot(0), :], rx_hi[f, slot(1), :]
        coarse = {x: fy[f, slot(x), :] for x in (0, 2, 4, 6)}
        mixed = rx_hi[f, slot(2), :]
        coarse[-4], coarse[8], coarse[12] = rx_lo[f, slot(1), :], mixed, pltpu.roll(mixed, 7, 0)
        for x in range(LX):
            if x % 2 == 1:
                coef[f, x] = fine[x] - predicted(fine[x - 1], fine[x + 1], fine[x - 3], fine[x + 3])
                continue
            value = coarse[x]
            if x % 4 == 2:
                value = value - predicted(coarse[x - 2], coarse[x + 2], coarse[x - 6], coarse[x + 6])
            coef[f, x] = jnp.where(even, value, fine[x])
    store_coef = pltpu.make_async_copy(coef, o_coef, local_sem.at[4])
    store_coef.start()

    for copy in halos + lifts[0] + lifts[1] + x_copies:
        copy.wait_send()
    for i in range(3):
        max_sent(i)
    store_state.wait()
    store_reg.wait()
    store_coef.wait()


def deliver(*refs):
    sources, targets, stages, sems = refs[:3], refs[3:6], refs[6:9], refs[9]
    loads = [pltpu.make_async_copy(sources[i], stages[i], sems.at[i]) for i in range(3)]
    stores = [pltpu.make_async_copy(stages[i], targets[i], sems.at[3 + i]) for i in range(3)]
    for load in loads:
        load.start()
    for load, store in zip(loads, stores):
        load.wait()
        store.start()
    for store in stores:
        store.wait()


def solution(mesh):
    sizes = (mesh.shape["gx"], mesh.shape["gy"], mesh.shape["gz"])
    spec = P(None, "gx", "gy", "gz")
    any_space = pl.BlockSpec(memory_space=pl.ANY)

    def vmem(*shape):
        return pltpu.VMEM(shape, F32)

    plane = (8, LZ)
    total = sizes[0] // 2 + sizes[1] + 2 * sizes[2]
    scratch = [
        vmem(NF, LX, *plane),
        vmem(NF, LX, *plane),
        vmem(NF, SPARE + 8, LZ),
        vmem(NF, SPARE, LZ),
        vmem(NF, *plane),
        vmem(NF, *plane),
        vmem(NF, *plane),
        vmem(NF, (LX + 2) * 8, LZ),
        vmem(NF, (LX + 1) * 8, LZ),
        vmem(NF, LX, *plane),
        vmem(NF, LX, *plane),
        vmem(NF, LX * 8, LZ),
        vmem(NF, (LX + 2) * 8, LZ),
        vmem(2, NF, 16, LZ),
        vmem(2, NF, 40, LZ),
        vmem(2, NF, 64, LZ),
        vmem(2, 16, LZ),
        vmem(2, 24, LZ),
        vmem(2, 16, LZ),
        vmem(2, 24, LZ),
        vmem(2, NF, *plane),
        vmem(2, 6, NF, *plane),
        vmem(2, 64, LZ),
        vmem(2, 64, LZ),
        vmem(2, 16, LZ),
        vmem(2, LX, *plane),
        vmem(sizes[0] // 2, 1, LZ),
        vmem(sizes[1], 1, LZ),
        vmem(2 * sizes[2], 1, LZ),
        pltpu.SemaphoreType.DMA((5,)),
        pltpu.SemaphoreType.DMA((6,)),
        pltpu.SemaphoreType.DMA((6,)),
        pltpu.SemaphoreType.DMA((total,)),
        pltpu.SemaphoreType.DMA((total,)),
        pltpu.SemaphoreType.DMA((18,)),
        pltpu.SemaphoreType.DMA((18,)),
    ]

    def local(state, register):
        block = jax.ShapeDtypeStruct(state.shape, F32)
        shapes = (block, block, jax.ShapeDtypeStruct((2,) + state.shape[1:], F32))
        results = pl.pallas_call(
            functools.partial(kernel, sizes),
            out_shape=shapes,
            in_specs=[any_space] * 2,
            out_specs=(any_space,) * 3,
            scratch_shapes=scratch,
            compiler_params=pltpu.CompilerParams(collective_id=0, has_side_effects=True),
        )(state, register)
        return pl.pallas_call(
            deliver,
            out_shape=shapes,
            in_specs=[any_space] * 3,
            out_specs=(any_space,) * 3,
            scratch_shapes=[pltpu.VMEM(shape.shape, F32) for shape in shapes] + [pltpu.SemaphoreType.DMA((6,))],
        )(*results)

    return jax.shard_map(local, mesh=mesh, in_specs=(spec, spec), out_specs=(spec,) * 3, check_vma=False)
```

```python
import functools

import jax
import jax.numpy as jnp
from jax import lax
from jax.experimental import pallas as pl
from jax.experimental.pallas import tpu as pltpu
from jax.sharding import PartitionSpec as P

F32 = jnp.float32
CFL_NUMBER = 0.3
SECTION_DECAY = -5.0 / 9.0
SECTION_GAIN = 15.0 / 16.0
NF = 5
LX = 8
LZ = 128
SPARE = (LX + 6) * 8


def weno_pair(a, b, c, d, e):
    e1 = b - a
    e2 = c - b
    e3 = d - c
    e4 = e - d
    d0 = e2 - e1
    d1 = e3 - e2
    d2 = e4 - e3
    g0 = d0 + 2.0 * e2
    g1 = e2 + e3
    g2 = d2 - 2.0 * e3
    third = 13.0 / 3.0
    s0 = (third * d0) * d0 + g0 * g0 + 4e-6
    s1 = (third * d1) * d1 + g1 * g1 + 4e-6
    s2 = (third * d2) * d2 + g2 * g2 + 4e-6
    t0 = s0 * s0
    t1 = s1 * s1
    t2 = s2 * s2
    n0 = t1 * t2
    n1 = 6.0 * (t0 * t2)
    n2 = t0 * t1
    n0_three = 3.0 * n0
    n2_three = 3.0 * n2
    left_up = n0 * (5.0 * e2 - 2.0 * e1) + n1 * (2.0 * e3 + e2) + n2_three * (4.0 * e3 - e4)
    right_up = n2 * (5.0 * e3 - 2.0 * e4) + n1 * (2.0 * e2 + e3) + n0_three * (4.0 * e2 - e1)
    left = c + left_up / (6.0 * (n0 + n1 + n2_three))
    right = c - right_up / (6.0 * (n2 + n1 + n0_three))
    return left, right


def floored(face, lower, upper):
    return (
        jnp.maximum(face[0], 0.5 * jnp.minimum(lower[0], upper[0])),
        face[1],
        face[2],
        face[3],
        jnp.maximum(face[4], 0.5 * jnp.minimum(lower[1], upper[1])),
    )


def hlle(left, right, normal):
    def terms(s):
        rho, u, v, w, p = s
        sound = jnp.sqrt(1.4 * p / rho)
        energy = 2.5 * p + 0.5 * rho * (u * u + v * v + w * w)
        return (rho, rho * u, rho * v, rho * w, energy), s[normal], sound

    ul, nl, cl = terms(left)
    ur, nr, cr = terms(right)
    sm = jnp.minimum(jnp.minimum(nl - cl, nr - cr), 0.0)
    sp = jnp.maximum(jnp.maximum(nl + cl, nr + cr), 0.0)
    inv = 1.0 / (sp - sm)
    spi = sp * inv
    smi = sm * inv
    al = spi * (nl - sm)
    ar = smi * (sp - nr)
    pl_ = spi * left[4]
    pr_ = smi * right[4]
    flux = [al * ul[k] + ar * ur[k] for k in range(NF)]
    flux[normal] = flux[normal] + (pl_ - pr_)
    flux[4] = flux[4] + (pl_ * nl - pr_ * nr)
    return tuple(flux)


def kernel(
    sizes,
    state,
    register,
    o_state,
    o_reg,
    o_coef,
    st,
    rg,
    px,
    py,
    ez,
    ezl,
    ezh,
    sides_x,
    sides_y,
    flux_x,
    flux_y,
    fz,
    sn,
    rn,
    base,
    rate,
    ends,
    turned,
    around,
    sx_hi,
    sx_lo,
    rx_lo,
    rx_hi,
    sz,
    rz,
    fn,
    fy,
    fc,
    coef,
    mx,
    my,
    mz,
    local_sem,
    halo_send,
    halo_recv,
    max_send,
    max_recv,
    lift_send,
    lift_recv,
):
    nx, ny, nz = sizes
    ix = lax.axis_index("gx")
    iy = lax.axis_index("gy")
    iz = lax.axis_index("gz")

    def turned_by(i, k, n):
        k = k % n
        return i if k == 0 else jnp.where(i >= n - k, i - (n - k), i + k)

    def at(dx=0, dy=0, dz=0):
        return {"gx": turned_by(ix, dx, nx), "gy": turned_by(iy, dy, ny), "gz": turned_by(iz, dz, nz)}

    chips_z, half_y = nx // 2, ny // 2
    upper_half = jnp.where(ix >= chips_z, 1, 0)
    chip_z = ix - upper_half * chips_z
    core = lax.rem(iy, 2)
    chip_y = upper_half * half_y + lax.div(iy, 2)

    def plane_mate(k):
        return {"gx": ix, "gy": iy if k < nz else iy + 1 - 2 * core, "gz": turned_by(iz, k, nz)}

    def column_mate(k):
        y = turned_by(chip_y, k, 2 * half_y)
        half = jnp.where(y >= half_y, 1, 0)
        return {"gx": half * chips_z + chip_z, "gy": (y - half * half_y) * 2 + core, "gz": iz}

    def depth_mate(k):
        return {"gx": upper_half * chips_z + turned_by(chip_z, k, chips_z), "gy": iy, "gz": iz}

    groups = ((plane_mate, 2 * nz), (column_mate, 2 * half_y), (depth_mate, chips_z))

    def far_first(count):
        return sorted(range(1, count), key=lambda k: -min(k, count - k))

    orders = (sorted(range(1, 2 * nz), key=lambda k: -min(k % nz, nz - k % nz)), far_first(2 * half_y), far_first(chips_z))

    barrier = pltpu.get_barrier_semaphore()

    def greet(target):
        pl.semaphore_signal(barrier, inc=1, device_id=target, device_id_type=pl.DeviceIdType.MESH)

    load_state = pltpu.make_async_copy(state, st, local_sem.at[0])
    load_reg = pltpu.make_async_copy(register, rg, local_sem.at[1])
    load_state.start()
    load_reg.start()
    for (mate, _), order in reversed(list(zip(groups, orders))):
        for k in order:
            greet(mate(k))
    for target in (at(dx=-1), at(dx=1)):
        greet(target)
    for dy in (-1, 0, 1):
        for dz in (-1, 0, 1):
            if (dy, dz) != (0, 0):
                greet(at(dy=dy, dz=dz))
    partners = sum(count - 1 for _, count in groups) + 10

    lane = lax.broadcasted_iota(jnp.int32, (8, LZ), 1)
    row = lax.broadcasted_iota(jnp.int32, (8, LZ), 0)
    group = lane // 16
    inner = lane % 16

    load_state.wait()

    def make_primitives(x, top):
        rho = st[0, x]
        inv = 1.0 / rho
        u = st[1, x] * inv
        v = st[2, x] * inv
        w = st[3, x] * inv
        p = 0.4 * (st[4, x] - 0.5 * rho * (u * u + v * v + w * w))
        here = (rho, u, v, w, p)
        rows = pl.ds(pl.multiple_of((x + 3) * 8, 8), 8)
        for k in range(NF):
            px[k, rows, :] = here[k]
        speed = jnp.maximum(jnp.maximum(jnp.abs(u), jnp.abs(v)), jnp.abs(w)) + jnp.sqrt(1.4 * p * inv)
        return jnp.maximum(top, speed)

    zero = jnp.zeros((8, LZ), F32)
    top = lax.fori_loop(0, LX, make_primitives, zero, unroll=4)
    top = jnp.max(jnp.max(top, axis=0, keepdims=True), axis=1, keepdims=True)
    mz[0] = jnp.broadcast_to(top, (1, LZ))

    pl.semaphore_wait(barrier, partners)

    def remote(src, dst, send, recv, target):
        return pltpu.make_async_remote_copy(
            src_ref=src,
            dst_ref=dst,
            send_sem=send,
            recv_sem=recv,
            device_id=target,
            device_id_type=pl.DeviceIdType.MESH,
        )

    bases = (0, groups[0][1], groups[0][1] + groups[1][1])
    slots = (mz, my, mx)

    def max_copy(i, k):
        sem = bases[i] + k
        return remote(slots[i].at[0], slots[i].at[k], max_send.at[sem], max_recv.at[sem], groups[i][0](k))

    def max_start(i):
        for k in orders[i]:
            max_copy(i, k).start()

    def max_wait(i):
        best = slots[i][0]
        for k in reversed(orders[i]):
            max_copy(i, k).wait_recv()
            best = jnp.maximum(best, slots[i][k])
        return best

    def max_sent(i):
        for k in orders[i]:
            max_copy(i, k).wait_send()

    max_start(0)

    low, high = pl.ds(0, 24), pl.ds(88, 24)
    first, last = pl.ds(24, 24), pl.ds(64, 24)
    halos = [
        remote(ez, ezl, halo_send.at[0], halo_recv.at[0], at(dz=1)),
        remote(ez, ezh, halo_send.at[1], halo_recv.at[1], at(dz=-1)),
        remote(py.at[:, last, :], py.at[:, low, :], halo_send.at[2], halo_recv.at[2], at(dy=1)),
        remote(py.at[:, first, :], py.at[:, high, :], halo_send.at[3], halo_recv.at[3], at(dy=-1)),
        remote(px.at[:, last, :], px.at[:, low, :], halo_send.at[4], halo_recv.at[4], at(dx=1)),
        remote(px.at[:, first, :], px.at[:, high, :], halo_send.at[5], halo_recv.at[5], at(dx=-1)),
    ]
    halos[4].start()
    halos[5].start()

    def turn(y, _):
        rows = pl.ds(pl.multiple_of((y + 3) * 8, 8), 8)
        for k in range(NF):
            py[k, rows, :] = px[k, pl.ds(24 + y, 8, stride=8), :]
        return 0

    lax.fori_loop(0, LX, turn, 0, unroll=4)
    halos[2].start()
    halos[3].start()

    def pack_edges(x, edges):
        rows = pl.ds(pl.multiple_of((x + 3) * 8, 8), 8)
        return tuple(
            jnp.where(group == x, pltpu.roll(px[k, rows, :], 16 * x + 3, 1), edges[k]) for k in range(NF)
        )

    edges = lax.fori_loop(0, LX, pack_edges, (zero,) * NF, unroll=4)
    for k in range(NF):
        ez[k] = edges[k]
    halos[0].start()
    halos[1].start()

    def slot(i):
        return pl.ds(8 * i if isinstance(i, int) else pl.multiple_of(i * 8, 8), 8)

    def plane(v, k, x):
        return (base, rate)[v][k, slot(x), :]

    def lift_copies(v):
        def one(i, src, dst, target):
            return remote(src, dst, lift_send.at[8 * v + i], lift_recv.at[8 * v + i], target)

        to_hi, to_lo = pl.ds(0, 16), pl.ds(16, 24)
        copies = [
            one(0, turned.at[v, :, to_hi, :], around.at[v, :, to_hi, :], at(dy=1)),
            one(1, turned.at[v, :, to_lo, :], around.at[v, :, to_lo, :], at(dy=-1)),
        ]
        for i, (dy, dz) in enumerate(((1, 1), (1, -1), (-1, 1), (-1, -1), (0, 1), (0, -1))):
            copies.append(one(2 + i, sz.at[v], rz.at[v, i], at(dy=dy, dz=dz)))
        return copies

    lifts = [lift_copies(0), lift_copies(1)]
    for v in range(2):
        for k in range(NF):
            around[v, k, pl.ds(40, 24), :] = jnp.zeros((24, LZ), F32)

    def send_lift(v):
        source = (base, rate)[v]
        for k in range(NF):
            for i, y in enumerate((4, 6, 0, 2, 4)):
                turned[v, k, pl.ds(8 * i, 8), :] = source[k, pl.ds(y, 8, stride=8), :]
        lifts[v][0].start()
        lifts[v][1].start()

        def pack_ends(x, packed):
            return tuple(
                jnp.where(group == x, pltpu.roll(plane(v, k, x), 16 * x + 4, 1), packed[k]) for k in range(NF)
            )

        packed = lax.fori_loop(0, LX, pack_ends, (zero,) * NF, unroll=4)
        for k in range(NF):
            sz[v, k] = packed[k]
        for copy in lifts[v][2:]:
            copy.start()

    from_low = inner < 4

    def receive_lift(v):
        for copy in lifts[v]:
            copy.wait_recv()
        for k in range(NF):
            below = jnp.where(from_low, rz[v, 0, k], rz[v, 1, k])
            above = jnp.where(from_low, rz[v, 2, k], rz[v, 3, k])
            outer = jnp.where(row == 0, pltpu.roll(below, 4, 0), pltpu.roll(below, 3, 0))
            outer = jnp.where(row == 2, pltpu.roll(above, 2, 0), outer)
            outer = jnp.where(row == 3, pltpu.roll(above, 1, 0), outer)
            ends[v, k, pl.ds(0, 8), :] = jnp.where(from_low, rz[v, 4, k], rz[v, 5, k])
            ends[v, k, pl.ds(8, 8), :] = jnp.where(row == 4, above, outer)


    def cell_faces(padded, sides, j):
        for k in range(NF):
            a, b, c, d, e = (padded[k, slot(j + i), :] for i in range(5))
            sides[0, k, slot(j), :], sides[1, k, slot(j), :] = weno_pair(a, b, c, d, e)

    def face_flux(padded, sides, flux, normal, f):
        lower = padded[0, slot(f + 2), :], padded[4, slot(f + 2), :]
        upper = padded[0, slot(f + 3), :], padded[4, slot(f + 3), :]
        left = floored([sides[0, k, slot(f), :] for k in range(NF)], lower, upper)
        right = floored([sides[1, k, slot(f + 1), :] for k in range(NF)], lower, upper)
        for k, value in enumerate(hlle(left, right, normal)):
            flux[k, slot(f), :] = value

    def sweep_inner(padded, sides, flux, normal):
        def cells(i, _):
            cell_faces(padded, sides, 3 + i)
            cell_faces(padded, sides, 5 + i)
            return 0

        def faces(i, _):
            face_flux(padded, sides, flux, normal, 3 + i)
            return 0

        lax.fori_loop(0, 2, cells, 0)
        lax.fori_loop(0, 3, faces, 0)

    def sweep_outer(padded, sides, flux, normal):
        def cells(i, _):
            cell_faces(padded, sides, i)
            cell_faces(padded, sides, 7 + i)
            return 0

        def faces(i, _):
            face_flux(padded, sides, flux, normal, i)
            face_flux(padded, sides, flux, normal, 6 + i)
            return 0

        lax.fori_loop(0, 3, cells, 0)
        lax.fori_loop(0, 3, faces, 0)

    my[0] = max_wait(0)
    max_start(1)

    load_reg.wait()

    def make_base(x, _):
        for k in range(NF):
            base[k, slot(x), :] = st[k, x] + (SECTION_GAIN * SECTION_DECAY) * rg[k, x]
        return 0

    lax.fori_loop(0, LX, make_base, 0, unroll=4)
    send_lift(0)
    sweep_inner(px, sides_x, flux_x, 1)
    sweep_inner(py, sides_y, flux_y, 2)
    halos[0].wait_recv()
    halos[1].wait_recv()
    for k in range(NF):
        lower = jnp.where(inner < 3, ezl[k], ez[k])
        upper = pltpu.roll(jnp.where(inner < 3, ez[k], ezh[k]), 8, 1)
        px[k, pl.ds(SPARE, 8), :] = jnp.where(inner < 8, lower, upper)

    def z_faces(x, _):
        rows = pl.ds(pl.multiple_of((x + 3 + 3 * (x // LX)) * 8, 8), 8)
        left, right, cell, nxt = [], [], [], []
        for k in range(NF):
            c = px[k, rows, :]
            outside = pltpu.roll(jnp.where(inner < 3, ezl[k], ezh[k]), lax.rem(253 - 16 * x, LZ), 1)
            a = pltpu.roll(jnp.where(lane >= LZ - 2, outside, c), 2, 1)
            b = pltpu.roll(jnp.where(lane >= LZ - 1, outside, c), 1, 1)
            d = pltpu.roll(jnp.where(lane < 1, outside, c), LZ - 1, 1)
            e = pltpu.roll(jnp.where(lane < 2, outside, c), LZ - 2, 1)
            lk, rk = weno_pair(a, b, c, d, e)
            left.append(lk)
            right.append(pltpu.roll(rk, LZ - 1, 1))
            cell.append(c)
            nxt.append(d)
        sides = (cell[0], cell[4]), (nxt[0], nxt[4])
        flux = hlle(floored(left, *sides), floored(right, *sides), 3)
        out = pl.ds(pl.multiple_of(x * 8, 8), 8)
        for k in range(NF):
            fz[k, out, :] = flux[k]
        return 0

    lax.fori_loop(0, LX + 1, z_faces, 0)
    for k in range(NF):
        tail = fz[k, pl.ds(64, 8), :]
        fz[k, pl.ds(64, 8), :] = jnp.where(inner == 11, pltpu.roll(tail, 9, 1), tail)

    halos[2].wait_recv()
    halos[3].wait_recv()
    sweep_outer(py, sides_y, flux_y, 2)
    mx[0] = max_wait(1)
    max_start(2)

    def make_rate(x, _):
        for k in range(NF):
            faces = fz[k, slot(x), :]
            tips = pltpu.roll(fz[k, pl.ds(64, 8), :], 117 - 16 * x, 1)
            upper = jnp.where(lane == LZ - 1, tips, faces)
            lower = jnp.where(lane == 0, tips, pltpu.roll(faces, 1, 1))
            upper_y = flux_y[k, pl.ds(8 + x, 8, stride=8), :]
            lower_y = flux_y[k, pl.ds(x, 8, stride=8), :]
            rate[k, slot(x), :] = (lower - upper) + (lower_y - upper_y)
        return 0

    lax.fori_loop(0, LX, make_rate, 0, unroll=4)
    halos[4].wait_recv()
    halos[5].wait_recv()
    sweep_outer(px, sides_x, flux_x, 1)

    def finish_rate(x, _):
        for k in range(NF):
            rate[k, slot(x), :] = rate[k, slot(x), :] + (flux_x[k, slot(x), :] - flux_x[k, slot(x + 1), :])
        return 0

    lax.fori_loop(0, LX, finish_rate, 0, unroll=4)
    send_lift(1)
    receive_lift(0)
    receive_lift(1)

    fastest = max_wait(2)
    step = jnp.broadcast_to(CFL_NUMBER / fastest, (8, LZ))
    gain = SECTION_GAIN * step

    def pressure(new):
        square = new[1] * new[1] + new[2] * new[2] + new[3] * new[3]
        return 0.4 * (new[4] - 0.5 * square / new[0])

    for j in range(2):
        new = [ends[0, k, slot(j), :] + gain * ends[1, k, slot(j), :] for k in range(NF)]
        fc[0, slot(j), :] = pressure(new)
        fc[1, slot(j), :] = new[0]

    def after(x):
        new = [plane(0, k, x) + gain * plane(1, k, x) for k in range(NF)]
        return pressure(new), new[0]

    def after_around(x):
        rows = pl.ds(x, 8, stride=8)
        new = [around[0, k, rows, :] + gain * around[1, k, rows, :] for k in range(NF)]
        return pressure(new), new[0]

    odd_lane = lane % 2 == 1
    mid_lane = lane % 4 == 2
    odd_row = row % 2 == 1
    mid_row = row % 4 == 2

    def predicted(down1, up1, down3, up3):
        return (9.0 * (down1 + up1) - (down3 + up3)) * 0.0625

    def fine_z(c, ends):
        up1 = pltpu.roll(jnp.where(lane < 1, ends, c), LZ - 1, 1)
        up3 = pltpu.roll(jnp.where(lane < 3, ends, c), LZ - 3, 1)
        down1 = pltpu.roll(c, 1, 1)
        down3 = pltpu.roll(jnp.where(lane >= LZ - 3, ends, c), 3, 1)
        return jnp.where(odd_lane, c - predicted(down1, up1, down3, up3), c)

    def coarse_z(c, ends):
        up2 = pltpu.roll(jnp.where(lane < 2, ends, c), LZ - 2, 1)
        up6 = pltpu.roll(jnp.where(lane < 6, ends, c), LZ - 6, 1)
        down2 = pltpu.roll(c, 2, 1)
        down6 = pltpu.roll(jnp.where(lane >= LZ - 6, ends, c), 6, 1)
        return jnp.where(mid_lane, c - predicted(down2, up2, down6, up6), c)

    def fine_y(c, outer):
        down1 = pltpu.roll(c, 1, 0)
        down3 = jnp.where(row == 1, outer, pltpu.roll(c, 3, 0))
        up1 = jnp.where(row == 7, pltpu.roll(outer, 5, 0), pltpu.roll(c, 7, 0))
        up3 = jnp.where(row == 7, pltpu.roll(outer, 4, 0), pltpu.roll(c, 5, 0))
        up3 = jnp.where(row == 5, pltpu.roll(outer, 3, 0), up3)
        return jnp.where(odd_row, c - predicted(down1, up1, down3, up3), c)

    def coarse_y(c, outer):
        down2 = pltpu.roll(c, 2, 0)
        further = pltpu.roll(c, 6, 0)
        beyond = pltpu.roll(outer, 2, 0)
        up2 = jnp.where(row == 6, pltpu.roll(outer, 4, 0), further)
        down6 = jnp.where(row == 2, beyond, further)
        up6 = jnp.where(row == 2, outer, beyond)
        return jnp.where(mid_row, c - predicted(down2, up2, down6, up6), c)

    def lift_zy(x, out, along_z, along_y):
        cells, outer = after(x), after_around(x)
        for f in range(2):
            tips = pltpu.roll(fc[f, slot(0), :], (252 - 16 * x) % LZ, 1)
            tips_outer = pltpu.roll(fc[f, slot(1), :], (252 - 16 * x) % LZ, 1)
            out[f, slot(x), :] = along_y(along_z(cells[f], tips), along_z(outer[f], tips_outer))

    def lift_fine(x):
        lift_zy(x, fn, fine_z, fine_y)

    def lift_coarse(x):
        lift_zy(x, fy, coarse_z, coarse_y)

    to_high = remote(sx_hi, rx_lo, lift_send.at[16], lift_recv.at[16], at(dx=1))
    to_low = remote(sx_lo, rx_hi, lift_send.at[17], lift_recv.at[17], at(dx=-1))
    lift_fine(6)
    lift_coarse(4)
    for f in range(2):
        sx_hi[f, slot(0), :] = fn[f, slot(6), :]
        sx_hi[f, slot(1), :] = fy[f, slot(4), :]
    to_high.start()
    lift_fine(0)
    lift_fine(2)
    lift_coarse(0)
    for f in range(2):
        sx_lo[f, slot(0), :] = fn[f, slot(0), :]
        sx_lo[f, slot(1), :] = fn[f, slot(2), :]
        sx_lo[f, slot(2), :] = jnp.where(odd_row, pltpu.roll(fy[f, slot(4), :], 1, 0), fy[f, slot(0), :])
    to_low.start()

    def update(x, _):
        for k in range(NF):
            r = SECTION_DECAY * rg[k, x] + step * plane(1, k, x)
            rn[k, x] = r
            sn[k, x] = st[k, x] + SECTION_GAIN * r
        return 0

    lax.fori_loop(0, LX, update, 0, unroll=4)
    store_state = pltpu.make_async_copy(sn, o_state, local_sem.at[2])
    store_reg = pltpu.make_async_copy(rn, o_reg, local_sem.at[3])
    store_state.start()
    store_reg.start()

    for x in (4, 1, 3, 5, 7):
        lift_fine(x)
    for x in (2, 6):
        lift_coarse(x)
    for copy in halos + lifts[0] + lifts[1]:
        copy.wait_send()
    for i in range(3):
        max_sent(i)

    to_high.wait_recv()
    to_low.wait_recv()
    even = jnp.logical_and(row % 2 == 0, lane % 2 == 0)
    for f in range(2):
        fine = {x: fn[f, slot(x), :] for x in range(LX)}
        fine[-2], fine[8], fine[10] = rx_lo[f, slot(0), :], rx_hi[f, slot(0), :], rx_hi[f, slot(1), :]
        coarse = {x: fy[f, slot(x), :] for x in (0, 2, 4, 6)}
        mixed = rx_hi[f, slot(2), :]
        coarse[-4], coarse[8], coarse[12] = rx_lo[f, slot(1), :], mixed, pltpu.roll(mixed, 7, 0)
        for x in range(LX):
            if x % 2 == 1:
                coef[f, x] = fine[x] - predicted(fine[x - 1], fine[x + 1], fine[x - 3], fine[x + 3])
                continue
            value = coarse[x]
            if x % 4 == 2:
                value = value - predicted(coarse[x - 2], coarse[x + 2], coarse[x - 6], coarse[x + 6])
            coef[f, x] = jnp.where(even, value, fine[x])
    store_coef = pltpu.make_async_copy(coef, o_coef, local_sem.at[4])
    store_coef.start()

    to_high.wait_send()
    to_low.wait_send()
    store_state.wait()
    store_reg.wait()
    store_coef.wait()


def deliver(*refs):
    sources, targets, stages, sems = refs[:3], refs[3:6], refs[6:9], refs[9]
    loads = [pltpu.make_async_copy(sources[i], stages[i], sems.at[i]) for i in range(3)]
    stores = [pltpu.make_async_copy(stages[i], targets[i], sems.at[3 + i]) for i in range(3)]
    for load in loads:
        load.start()
    for load, store in zip(loads, stores):
        load.wait()
        store.start()
    for store in stores:
        store.wait()


def solution(mesh):
    sizes = (mesh.shape["gx"], mesh.shape["gy"], mesh.shape["gz"])
    spec = P(None, "gx", "gy", "gz")
    any_space = pl.BlockSpec(memory_space=pl.ANY)

    def vmem(*shape):
        return pltpu.VMEM(shape, F32)

    plane = (8, LZ)
    total = sizes[0] // 2 + sizes[1] + 2 * sizes[2]
    scratch = [
        vmem(NF, LX, *plane),
        vmem(NF, LX, *plane),
        vmem(NF, SPARE + 8, LZ),
        vmem(NF, SPARE, LZ),
        vmem(NF, *plane),
        vmem(NF, *plane),
        vmem(NF, *plane),
        vmem(2, NF, (LX + 2) * 8, LZ),
        vmem(2, NF, (LX + 2) * 8, LZ),
        vmem(NF, (LX + 1) * 8, LZ),
        vmem(NF, (LX + 1) * 8, LZ),
        vmem(NF, (LX + 1) * 8, LZ),
        vmem(NF, LX, *plane),
        vmem(NF, LX, *plane),
        vmem(NF, LX * 8, LZ),
        vmem(NF, LX * 8, LZ),
        vmem(2, NF, 16, LZ),
        vmem(2, NF, 40, LZ),
        vmem(2, NF, 64, LZ),
        vmem(2, 16, LZ),
        vmem(2, 24, LZ),
        vmem(2, 16, LZ),
        vmem(2, 24, LZ),
        vmem(2, NF, *plane),
        vmem(2, 6, NF, *plane),
        vmem(2, 64, LZ),
        vmem(2, 64, LZ),
        vmem(2, 16, LZ),
        vmem(2, LX, *plane),
        vmem(sizes[0] // 2, 1, LZ),
        vmem(sizes[1], 1, LZ),
        vmem(2 * sizes[2], 1, LZ),
        pltpu.SemaphoreType.DMA((5,)),
        pltpu.SemaphoreType.DMA((6,)),
        pltpu.SemaphoreType.DMA((6,)),
        pltpu.SemaphoreType.DMA((total,)),
        pltpu.SemaphoreType.DMA((total,)),
        pltpu.SemaphoreType.DMA((18,)),
        pltpu.SemaphoreType.DMA((18,)),
    ]

    def local(state, register):
        block = jax.ShapeDtypeStruct(state.shape, F32)
        shapes = (block, block, jax.ShapeDtypeStruct((2,) + state.shape[1:], F32))
        results = pl.pallas_call(
            functools.partial(kernel, sizes),
            out_shape=shapes,
            in_specs=[any_space] * 2,
            out_specs=(any_space,) * 3,
            scratch_shapes=scratch,
            compiler_params=pltpu.CompilerParams(collective_id=0, has_side_effects=True),
        )(state, register)
        return pl.pallas_call(
            deliver,
            out_shape=shapes,
            in_specs=[any_space] * 3,
            out_specs=(any_space,) * 3,
            scratch_shapes=[pltpu.VMEM(shape.shape, F32) for shape in shapes] + [pltpu.SemaphoreType.DMA((6,))],
        )(*results)

    return jax.shard_map(local, mesh=mesh, in_specs=(spec, spec), out_specs=(spec,) * 3, check_vma=False)
```

```python
import functools

import jax
import jax.numpy as jnp
from jax import lax
from jax.experimental import pallas as pl
from jax.experimental.pallas import tpu as pltpu
from jax.sharding import PartitionSpec as P

F32 = jnp.float32
CFL_NUMBER = 0.3
SECTION_DECAY = -5.0 / 9.0
SECTION_GAIN = 15.0 / 16.0
NF = 5
LX = 8
LZ = 128
SPARE = (LX + 6) * 8


def weno_pair(a, b, c, d, e):
    e1 = b - a
    e2 = c - b
    e3 = d - c
    e4 = e - d
    d0 = e2 - e1
    d1 = e3 - e2
    d2 = e4 - e3
    g0 = d0 + 2.0 * e2
    g1 = e2 + e3
    g2 = d2 - 2.0 * e3
    third = 13.0 / 3.0
    s0 = (third * d0) * d0 + g0 * g0 + 4e-6
    s1 = (third * d1) * d1 + g1 * g1 + 4e-6
    s2 = (third * d2) * d2 + g2 * g2 + 4e-6
    t0 = s0 * s0
    t1 = s1 * s1
    t2 = s2 * s2
    n0 = t1 * t2
    n1 = 6.0 * (t0 * t2)
    n2 = t0 * t1
    n0_three = 3.0 * n0
    n2_three = 3.0 * n2
    left_up = n0 * (5.0 * e2 - 2.0 * e1) + n1 * (2.0 * e3 + e2) + n2_three * (4.0 * e3 - e4)
    right_up = n2 * (5.0 * e3 - 2.0 * e4) + n1 * (2.0 * e2 + e3) + n0_three * (4.0 * e2 - e1)
    left = c + left_up / (6.0 * (n0 + n1 + n2_three))
    right = c - right_up / (6.0 * (n2 + n1 + n0_three))
    return left, right


def floored(face, lower, upper):
    return (
        jnp.maximum(face[0], 0.5 * jnp.minimum(lower[0], upper[0])),
        face[1],
        face[2],
        face[3],
        jnp.maximum(face[4], 0.5 * jnp.minimum(lower[1], upper[1])),
    )


def hlle(left, right, normal):
    def terms(s):
        rho, u, v, w, p = s
        sound = jnp.sqrt(1.4 * p / rho)
        energy = 2.5 * p + 0.5 * rho * (u * u + v * v + w * w)
        return (rho, rho * u, rho * v, rho * w, energy), s[normal], sound

    ul, nl, cl = terms(left)
    ur, nr, cr = terms(right)
    sm = jnp.minimum(jnp.minimum(nl - cl, nr - cr), 0.0)
    sp = jnp.maximum(jnp.maximum(nl + cl, nr + cr), 0.0)
    inv = 1.0 / (sp - sm)
    spi = sp * inv
    smi = sm * inv
    al = spi * (nl - sm)
    ar = smi * (sp - nr)
    pl_ = spi * left[4]
    pr_ = smi * right[4]
    flux = [al * ul[k] + ar * ur[k] for k in range(NF)]
    flux[normal] = flux[normal] + (pl_ - pr_)
    flux[4] = flux[4] + (pl_ * nl - pr_ * nr)
    return tuple(flux)


def kernel(
    sizes,
    state,
    register,
    o_state,
    o_reg,
    o_coef,
    st,
    rg,
    px,
    py,
    ez,
    ezl,
    ezh,
    sides_x,
    sides_y,
    flux_x,
    flux_y,
    fz,
    sn,
    rn,
    base,
    rate,
    ends,
    turned,
    around,
    sx_hi,
    sx_lo,
    rx_lo,
    rx_hi,
    sz,
    rz,
    fn,
    fy,
    fc,
    coef,
    mx,
    my,
    mz,
    local_sem,
    halo_send,
    halo_recv,
    max_send,
    max_recv,
    lift_send,
    lift_recv,
    known,
):
    nx, ny, nz = sizes
    ix = lax.axis_index("gx")
    iy = lax.axis_index("gy")
    iz = lax.axis_index("gz")

    def turned_by(i, k, n):
        k = k % n
        return i if k == 0 else jnp.where(i >= n - k, i - (n - k), i + k)

    def at(dx=0, dy=0, dz=0):
        return {"gx": turned_by(ix, dx, nx), "gy": turned_by(iy, dy, ny), "gz": turned_by(iz, dz, nz)}

    chips_z, half_y = nx // 2, ny // 2
    upper_half = jnp.where(ix >= chips_z, 1, 0)
    chip_z = ix - upper_half * chips_z
    core = lax.rem(iy, 2)
    chip_y = upper_half * half_y + lax.div(iy, 2)

    def plane_mate(k):
        return {"gx": ix, "gy": iy if k < nz else iy + 1 - 2 * core, "gz": turned_by(iz, k, nz)}

    def column_mate(k):
        y = turned_by(chip_y, k, 2 * half_y)
        half = jnp.where(y >= half_y, 1, 0)
        return {"gx": half * chips_z + chip_z, "gy": (y - half * half_y) * 2 + core, "gz": iz}

    def depth_mate(k):
        return {"gx": upper_half * chips_z + turned_by(chip_z, k, chips_z), "gy": iy, "gz": iz}

    groups = ((plane_mate, 2 * nz), (column_mate, 2 * half_y), (depth_mate, chips_z))

    def far_first(count):
        return sorted(range(1, count), key=lambda k: -min(k, count - k))

    orders = (sorted(range(1, 2 * nz), key=lambda k: -min(k % nz, nz - k % nz)), far_first(2 * half_y), far_first(chips_z))

    barrier = pltpu.get_barrier_semaphore()

    def greet(target):
        pl.semaphore_signal(barrier, inc=1, device_id=target, device_id_type=pl.DeviceIdType.MESH)

    load_state = pltpu.make_async_copy(state, st, local_sem.at[0])
    load_reg = pltpu.make_async_copy(register, rg, local_sem.at[1])
    load_state.start()
    load_reg.start()
    near = ((depth_mate, chips_z), (column_mate, 2 * half_y))
    offsets = [(mate, k) for mate, n in near for k in sorted({2 % n, 1 % n, n - 1, (n - 2) % n} - {0})]
    offsets += [(plane_mate, k) for k in orders[0]]
    for mate, k in offsets:
        greet(mate(k))
    for target in (at(dx=-1), at(dx=1)):
        greet(target)
    for dy in (-1, 0, 1):
        for dz in (-1, 0, 1):
            if (dy, dz) != (0, 0):
                greet(at(dy=dy, dz=dz))
    partners = len(offsets) + 10

    lane = lax.broadcasted_iota(jnp.int32, (8, LZ), 1)
    row = lax.broadcasted_iota(jnp.int32, (8, LZ), 0)
    group = lane // 16
    inner = lane % 16

    load_state.wait()

    def make_primitives(x, top):
        rho = st[0, x]
        inv = 1.0 / rho
        u = st[1, x] * inv
        v = st[2, x] * inv
        w = st[3, x] * inv
        p = 0.4 * (st[4, x] - 0.5 * rho * (u * u + v * v + w * w))
        here = (rho, u, v, w, p)
        rows = pl.ds(pl.multiple_of((x + 3) * 8, 8), 8)
        for k in range(NF):
            px[k, rows, :] = here[k]
        speed = jnp.maximum(jnp.maximum(jnp.abs(u), jnp.abs(v)), jnp.abs(w)) + jnp.sqrt(1.4 * p * inv)
        return jnp.maximum(top, speed)

    zero = jnp.zeros((8, LZ), F32)
    top = lax.fori_loop(0, LX, make_primitives, zero, unroll=4)
    top = jnp.max(jnp.max(top, axis=0, keepdims=True), axis=1, keepdims=True)
    mz[0] = jnp.broadcast_to(top, (1, LZ))

    pl.semaphore_wait(barrier, partners)

    def remote(src, dst, send, recv, target):
        return pltpu.make_async_remote_copy(
            src_ref=src,
            dst_ref=dst,
            send_sem=send,
            recv_sem=recv,
            device_id=target,
            device_id_type=pl.DeviceIdType.MESH,
        )

    bases = (0, groups[0][1], groups[0][1] + groups[1][1])
    slots = (mz, my, mx)

    def max_copy(i, k):
        sem = bases[i] + k
        return remote(slots[i].at[0], slots[i].at[k], max_send.at[sem], max_recv.at[sem], groups[i][0](k))

    def max_start(i):
        for k in orders[i]:
            max_copy(i, k).start()

    def max_wait(i):
        best = slots[i][0]
        for k in reversed(orders[i]):
            max_copy(i, k).wait_recv()
            best = jnp.maximum(best, slots[i][k])
        return best

    def max_sent(i):
        for k in orders[i]:
            max_copy(i, k).wait_send()

    low, high = pl.ds(0, 24), pl.ds(88, 24)
    first, last = pl.ds(24, 24), pl.ds(64, 24)
    halos = [
        remote(ez, ezl, halo_send.at[0], halo_recv.at[0], at(dz=1)),
        remote(ez, ezh, halo_send.at[1], halo_recv.at[1], at(dz=-1)),
        remote(py.at[:, last, :], py.at[:, low, :], halo_send.at[2], halo_recv.at[2], at(dy=1)),
        remote(py.at[:, first, :], py.at[:, high, :], halo_send.at[3], halo_recv.at[3], at(dy=-1)),
        remote(px.at[:, last, :], px.at[:, low, :], halo_send.at[4], halo_recv.at[4], at(dx=1)),
        remote(px.at[:, first, :], px.at[:, high, :], halo_send.at[5], halo_recv.at[5], at(dx=-1)),
    ]
    halos[4].start()
    halos[5].start()
    max_start(0)

    def hand_on(mate, n, sem):
        for k in (2, n - 2):
            pl.semaphore_signal(known.at[sem], inc=1, device_id=mate(k), device_id_type=pl.DeviceIdType.MESH)

    def heard(sem):
        pl.semaphore_wait(known.at[sem], 2)

    far_y, far_z, farther_z = half_y > 2, chips_z > 5, chips_z > 9
    if far_z:
        hand_on(depth_mate, chips_z, 1)
    if far_y:
        hand_on(column_mate, 2 * half_y, 0)

    def turn(y, _):
        rows = pl.ds(pl.multiple_of((y + 3) * 8, 8), 8)
        for k in range(NF):
            py[k, rows, :] = px[k, pl.ds(24 + y, 8, stride=8), :]
        return 0

    lax.fori_loop(0, LX, turn, 0, unroll=4)
    halos[2].start()
    halos[3].start()

    def pack_edges(x, edges):
        rows = pl.ds(pl.multiple_of((x + 3) * 8, 8), 8)
        return tuple(
            jnp.where(group == x, pltpu.roll(px[k, rows, :], 16 * x + 3, 1), edges[k]) for k in range(NF)
        )

    edges = lax.fori_loop(0, LX, pack_edges, (zero,) * NF, unroll=4)
    for k in range(NF):
        ez[k] = edges[k]
    halos[0].start()
    halos[1].start()

    def slot(i):
        return pl.ds(8 * i if isinstance(i, int) else pl.multiple_of(i * 8, 8), 8)

    def plane(v, k, x):
        return (base, rate)[v][k, slot(x), :]

    def lift_copies(v):
        def one(i, src, dst, target):
            return remote(src, dst, lift_send.at[8 * v + i], lift_recv.at[8 * v + i], target)

        to_hi, to_lo = pl.ds(0, 16), pl.ds(16, 24)
        copies = [
            one(0, turned.at[v, :, to_hi, :], around.at[v, :, to_hi, :], at(dy=1)),
            one(1, turned.at[v, :, to_lo, :], around.at[v, :, to_lo, :], at(dy=-1)),
        ]
        for i, (dy, dz) in enumerate(((1, 1), (1, -1), (-1, 1), (-1, -1), (0, 1), (0, -1))):
            copies.append(one(2 + i, sz.at[v], rz.at[v, i], at(dy=dy, dz=dz)))
        return copies

    lifts = [lift_copies(0), lift_copies(1)]
    for v in range(2):
        for k in range(NF):
            around[v, k, pl.ds(40, 24), :] = jnp.zeros((24, LZ), F32)

    def send_lift(v):
        source = (base, rate)[v]
        for k in range(NF):
            for i, y in enumerate((4, 6, 0, 2, 4)):
                turned[v, k, pl.ds(8 * i, 8), :] = source[k, pl.ds(y, 8, stride=8), :]
        lifts[v][0].start()
        lifts[v][1].start()

        def pack_ends(x, packed):
            return tuple(
                jnp.where(group == x, pltpu.roll(plane(v, k, x), 16 * x + 4, 1), packed[k]) for k in range(NF)
            )

        packed = lax.fori_loop(0, LX, pack_ends, (zero,) * NF, unroll=4)
        for k in range(NF):
            sz[v, k] = packed[k]
        for copy in lifts[v][2:]:
            copy.start()

    from_low = inner < 4

    def receive_lift(v):
        for copy in lifts[v]:
            copy.wait_recv()
        for k in range(NF):
            below = jnp.where(from_low, rz[v, 0, k], rz[v, 1, k])
            above = jnp.where(from_low, rz[v, 2, k], rz[v, 3, k])
            outer = jnp.where(row == 0, pltpu.roll(below, 4, 0), pltpu.roll(below, 3, 0))
            outer = jnp.where(row == 2, pltpu.roll(above, 2, 0), outer)
            outer = jnp.where(row == 3, pltpu.roll(above, 1, 0), outer)
            ends[v, k, pl.ds(0, 8), :] = jnp.where(from_low, rz[v, 4, k], rz[v, 5, k])
            ends[v, k, pl.ds(8, 8), :] = jnp.where(row == 4, above, outer)


    def cell_faces(padded, sides, j):
        for k in range(NF):
            a, b, c, d, e = (padded[k, slot(j + i), :] for i in range(5))
            sides[0, k, slot(j), :], sides[1, k, slot(j), :] = weno_pair(a, b, c, d, e)

    def face_flux(padded, sides, flux, normal, f):
        lower = padded[0, slot(f + 2), :], padded[4, slot(f + 2), :]
        upper = padded[0, slot(f + 3), :], padded[4, slot(f + 3), :]
        left = floored([sides[0, k, slot(f), :] for k in range(NF)], lower, upper)
        right = floored([sides[1, k, slot(f + 1), :] for k in range(NF)], lower, upper)
        for k, value in enumerate(hlle(left, right, normal)):
            flux[k, slot(f), :] = value

    def sweep_inner(padded, sides, flux, normal):
        def cells(i, _):
            cell_faces(padded, sides, 3 + i)
            cell_faces(padded, sides, 5 + i)
            return 0

        def faces(i, _):
            face_flux(padded, sides, flux, normal, 3 + i)
            return 0

        lax.fori_loop(0, 2, cells, 0)
        lax.fori_loop(0, 3, faces, 0)

    def sweep_outer(padded, sides, flux, normal):
        def cells(i, _):
            cell_faces(padded, sides, i)
            cell_faces(padded, sides, 7 + i)
            return 0

        def faces(i, _):
            face_flux(padded, sides, flux, normal, i)
            face_flux(padded, sides, flux, normal, 6 + i)
            return 0

        lax.fori_loop(0, 3, cells, 0)
        lax.fori_loop(0, 3, faces, 0)

    if far_z:
        heard(1)
    if farther_z:
        hand_on(depth_mate, chips_z, 2)
    my[0] = max_wait(0)
    if far_y:
        heard(0)
    max_start(1)

    load_reg.wait()

    def make_base(x, _):
        for k in range(NF):
            base[k, slot(x), :] = st[k, x] + (SECTION_GAIN * SECTION_DECAY) * rg[k, x]
        return 0

    lax.fori_loop(0, LX, make_base, 0, unroll=4)
    send_lift(0)
    sweep_inner(px, sides_x, flux_x, 1)
    sweep_inner(py, sides_y, flux_y, 2)
    halos[0].wait_recv()
    halos[1].wait_recv()
    for k in range(NF):
        lower = jnp.where(inner < 3, ezl[k], ez[k])
        upper = pltpu.roll(jnp.where(inner < 3, ez[k], ezh[k]), 8, 1)
        px[k, pl.ds(SPARE, 8), :] = jnp.where(inner < 8, lower, upper)

    def z_faces(x, _):
        rows = pl.ds(pl.multiple_of((x + 3 + 3 * (x // LX)) * 8, 8), 8)
        left, right, cell, nxt = [], [], [], []
        for k in range(NF):
            c = px[k, rows, :]
            outside = pltpu.roll(jnp.where(inner < 3, ezl[k], ezh[k]), lax.rem(253 - 16 * x, LZ), 1)
            a = pltpu.roll(jnp.where(lane >= LZ - 2, outside, c), 2, 1)
            b = pltpu.roll(jnp.where(lane >= LZ - 1, outside, c), 1, 1)
            d = pltpu.roll(jnp.where(lane < 1, outside, c), LZ - 1, 1)
            e = pltpu.roll(jnp.where(lane < 2, outside, c), LZ - 2, 1)
            lk, rk = weno_pair(a, b, c, d, e)
            left.append(lk)
            right.append(pltpu.roll(rk, LZ - 1, 1))
            cell.append(c)
            nxt.append(d)
        sides = (cell[0], cell[4]), (nxt[0], nxt[4])
        flux = hlle(floored(left, *sides), floored(right, *sides), 3)
        out = pl.ds(pl.multiple_of(x * 8, 8), 8)
        for k in range(NF):
            fz[k, out, :] = flux[k]
        return 0

    lax.fori_loop(0, LX + 1, z_faces, 0)
    for k in range(NF):
        tail = fz[k, pl.ds(64, 8), :]
        fz[k, pl.ds(64, 8), :] = jnp.where(inner == 11, pltpu.roll(tail, 9, 1), tail)

    halos[2].wait_recv()
    halos[3].wait_recv()
    sweep_outer(py, sides_y, flux_y, 2)

    def make_rate(x, _):
        for k in range(NF):
            faces = fz[k, slot(x), :]
            tips = pltpu.roll(fz[k, pl.ds(64, 8), :], 117 - 16 * x, 1)
            upper = jnp.where(lane == LZ - 1, tips, faces)
            lower = jnp.where(lane == 0, tips, pltpu.roll(faces, 1, 1))
            upper_y = flux_y[k, pl.ds(8 + x, 8, stride=8), :]
            lower_y = flux_y[k, pl.ds(x, 8, stride=8), :]
            rate[k, slot(x), :] = (lower - upper) + (lower_y - upper_y)
        return 0

    lax.fori_loop(0, LX, make_rate, 0, unroll=4)
    halos[4].wait_recv()
    halos[5].wait_recv()
    sweep_outer(px, sides_x, flux_x, 1)

    def finish_rate(x, _):
        for k in range(NF):
            rate[k, slot(x), :] = rate[k, slot(x), :] + (flux_x[k, slot(x), :] - flux_x[k, slot(x + 1), :])
        return 0

    lax.fori_loop(0, LX, finish_rate, 0, unroll=4)
    send_lift(1)
    mx[0] = max_wait(1)
    if farther_z:
        heard(2)
    max_start(2)
    receive_lift(0)
    receive_lift(1)

    fastest = max_wait(2)
    step = jnp.broadcast_to(CFL_NUMBER / fastest, (8, LZ))
    gain = SECTION_GAIN * step

    def pressure(new):
        square = new[1] * new[1] + new[2] * new[2] + new[3] * new[3]
        return 0.4 * (new[4] - 0.5 * square / new[0])

    for j in range(2):
        new = [ends[0, k, slot(j), :] + gain * ends[1, k, slot(j), :] for k in range(NF)]
        fc[0, slot(j), :] = pressure(new)
        fc[1, slot(j), :] = new[0]

    def after(x):
        new = [plane(0, k, x) + gain * plane(1, k, x) for k in range(NF)]
        return pressure(new), new[0]

    def after_around(x):
        rows = pl.ds(x, 8, stride=8)
        new = [around[0, k, rows, :] + gain * around[1, k, rows, :] for k in range(NF)]
        return pressure(new), new[0]

    odd_lane = lane % 2 == 1
    mid_lane = lane % 4 == 2
    odd_row = row % 2 == 1
    mid_row = row % 4 == 2

    def predicted(down1, up1, down3, up3):
        return (9.0 * (down1 + up1) - (down3 + up3)) * 0.0625

    def fine_z(c, ends):
        up1 = pltpu.roll(jnp.where(lane < 1, ends, c), LZ - 1, 1)
        up3 = pltpu.roll(jnp.where(lane < 3, ends, c), LZ - 3, 1)
        down1 = pltpu.roll(c, 1, 1)
        down3 = pltpu.roll(jnp.where(lane >= LZ - 3, ends, c), 3, 1)
        return jnp.where(odd_lane, c - predicted(down1, up1, down3, up3), c)

    def coarse_z(c, ends):
        up2 = pltpu.roll(jnp.where(lane < 2, ends, c), LZ - 2, 1)
        up6 = pltpu.roll(jnp.where(lane < 6, ends, c), LZ - 6, 1)
        down2 = pltpu.roll(c, 2, 1)
        down6 = pltpu.roll(jnp.where(lane >= LZ - 6, ends, c), 6, 1)
        return jnp.where(mid_lane, c - predicted(down2, up2, down6, up6), c)

    def fine_y(c, outer):
        down1 = pltpu.roll(c, 1, 0)
        down3 = jnp.where(row == 1, outer, pltpu.roll(c, 3, 0))
        up1 = jnp.where(row == 7, pltpu.roll(outer, 5, 0), pltpu.roll(c, 7, 0))
        up3 = jnp.where(row == 7, pltpu.roll(outer, 4, 0), pltpu.roll(c, 5, 0))
        up3 = jnp.where(row == 5, pltpu.roll(outer, 3, 0), up3)
        return jnp.where(odd_row, c - predicted(down1, up1, down3, up3), c)

    def coarse_y(c, outer):
        down2 = pltpu.roll(c, 2, 0)
        further = pltpu.roll(c, 6, 0)
        beyond = pltpu.roll(outer, 2, 0)
        up2 = jnp.where(row == 6, pltpu.roll(outer, 4, 0), further)
        down6 = jnp.where(row == 2, beyond, further)
        up6 = jnp.where(row == 2, outer, beyond)
        return jnp.where(mid_row, c - predicted(down2, up2, down6, up6), c)

    def lift_zy(x, out, along_z, along_y):
        cells, outer = after(x), after_around(x)
        for f in range(2):
            tips = pltpu.roll(fc[f, slot(0), :], (252 - 16 * x) % LZ, 1)
            tips_outer = pltpu.roll(fc[f, slot(1), :], (252 - 16 * x) % LZ, 1)
            out[f, slot(x), :] = along_y(along_z(cells[f], tips), along_z(outer[f], tips_outer))

    def lift_fine(x):
        lift_zy(x, fn, fine_z, fine_y)

    def lift_coarse(x):
        lift_zy(x, fy, coarse_z, coarse_y)

    to_high = remote(sx_hi, rx_lo, lift_send.at[16], lift_recv.at[16], at(dx=1))
    to_low = remote(sx_lo, rx_hi, lift_send.at[17], lift_recv.at[17], at(dx=-1))
    lift_fine(6)
    lift_coarse(4)
    for f in range(2):
        sx_hi[f, slot(0), :] = fn[f, slot(6), :]
        sx_hi[f, slot(1), :] = fy[f, slot(4), :]
    to_high.start()
    lift_fine(0)
    lift_fine(2)
    lift_coarse(0)
    for f in range(2):
        sx_lo[f, slot(0), :] = fn[f, slot(0), :]
        sx_lo[f, slot(1), :] = fn[f, slot(2), :]
        sx_lo[f, slot(2), :] = jnp.where(odd_row, pltpu.roll(fy[f, slot(4), :], 1, 0), fy[f, slot(0), :])
    to_low.start()

    def update(x, _):
        for k in range(NF):
            r = SECTION_DECAY * rg[k, x] + step * plane(1, k, x)
            rn[k, x] = r
            sn[k, x] = st[k, x] + SECTION_GAIN * r
        return 0

    lax.fori_loop(0, LX, update, 0, unroll=4)
    store_state = pltpu.make_async_copy(sn, o_state, local_sem.at[2])
    store_reg = pltpu.make_async_copy(rn, o_reg, local_sem.at[3])
    store_state.start()
    store_reg.start()

    for x in (4, 1, 3, 5, 7):
        lift_fine(x)
    for x in (2, 6):
        lift_coarse(x)
    for copy in halos + lifts[0] + lifts[1]:
        copy.wait_send()
    for i in range(3):
        max_sent(i)

    to_high.wait_recv()
    to_low.wait_recv()
    even = jnp.logical_and(row % 2 == 0, lane % 2 == 0)
    for f in range(2):
        fine = {x: fn[f, slot(x), :] for x in range(LX)}
        fine[-2], fine[8], fine[10] = rx_lo[f, slot(0), :], rx_hi[f, slot(0), :], rx_hi[f, slot(1), :]
        coarse = {x: fy[f, slot(x), :] for x in (0, 2, 4, 6)}
        mixed = rx_hi[f, slot(2), :]
        coarse[-4], coarse[8], coarse[12] = rx_lo[f, slot(1), :], mixed, pltpu.roll(mixed, 7, 0)
        for x in range(LX):
            if x % 2 == 1:
                coef[f, x] = fine[x] - predicted(fine[x - 1], fine[x + 1], fine[x - 3], fine[x + 3])
                continue
            value = coarse[x]
            if x % 4 == 2:
                value = value - predicted(coarse[x - 2], coarse[x + 2], coarse[x - 6], coarse[x + 6])
            coef[f, x] = jnp.where(even, value, fine[x])
    store_coef = pltpu.make_async_copy(coef, o_coef, local_sem.at[4])
    store_coef.start()

    to_high.wait_send()
    to_low.wait_send()
    store_state.wait()
    store_reg.wait()
    store_coef.wait()


def deliver(*refs):
    sources, targets, stages, sems = refs[:3], refs[3:6], refs[6:9], refs[9]
    loads = [pltpu.make_async_copy(sources[i], stages[i], sems.at[i]) for i in range(3)]
    stores = [pltpu.make_async_copy(stages[i], targets[i], sems.at[3 + i]) for i in range(3)]
    for load in loads:
        load.start()
    for load, store in zip(loads, stores):
        load.wait()
        store.start()
    for store in stores:
        store.wait()


def solution(mesh):
    sizes = (mesh.shape["gx"], mesh.shape["gy"], mesh.shape["gz"])
    spec = P(None, "gx", "gy", "gz")
    any_space = pl.BlockSpec(memory_space=pl.ANY)

    def vmem(*shape):
        return pltpu.VMEM(shape, F32)

    plane = (8, LZ)
    total = sizes[0] // 2 + sizes[1] + 2 * sizes[2]
    scratch = [
        vmem(NF, LX, *plane),
        vmem(NF, LX, *plane),
        vmem(NF, SPARE + 8, LZ),
        vmem(NF, SPARE, LZ),
        vmem(NF, *plane),
        vmem(NF, *plane),
        vmem(NF, *plane),
        vmem(2, NF, (LX + 2) * 8, LZ),
        vmem(2, NF, (LX + 2) * 8, LZ),
        vmem(NF, (LX + 1) * 8, LZ),
        vmem(NF, (LX + 1) * 8, LZ),
        vmem(NF, (LX + 1) * 8, LZ),
        vmem(NF, LX, *plane),
        vmem(NF, LX, *plane),
        vmem(NF, LX * 8, LZ),
        vmem(NF, LX * 8, LZ),
        vmem(2, NF, 16, LZ),
        vmem(2, NF, 40, LZ),
        vmem(2, NF, 64, LZ),
        vmem(2, 16, LZ),
        vmem(2, 24, LZ),
        vmem(2, 16, LZ),
        vmem(2, 24, LZ),
        vmem(2, NF, *plane),
        vmem(2, 6, NF, *plane),
        vmem(2, 64, LZ),
        vmem(2, 64, LZ),
        vmem(2, 16, LZ),
        vmem(2, LX, *plane),
        vmem(sizes[0] // 2, 1, LZ),
        vmem(sizes[1], 1, LZ),
        vmem(2 * sizes[2], 1, LZ),
        pltpu.SemaphoreType.DMA((5,)),
        pltpu.SemaphoreType.DMA((6,)),
        pltpu.SemaphoreType.DMA((6,)),
        pltpu.SemaphoreType.DMA((total,)),
        pltpu.SemaphoreType.DMA((total,)),
        pltpu.SemaphoreType.DMA((18,)),
        pltpu.SemaphoreType.DMA((18,)),
        pltpu.SemaphoreType.REGULAR((3,)),
    ]

    def local(state, register):
        block = jax.ShapeDtypeStruct(state.shape, F32)
        shapes = (block, block, jax.ShapeDtypeStruct((2,) + state.shape[1:], F32))
        results = pl.pallas_call(
            functools.partial(kernel, sizes),
            out_shape=shapes,
            in_specs=[any_space] * 2,
            out_specs=(any_space,) * 3,
            scratch_shapes=scratch,
            compiler_params=pltpu.CompilerParams(collective_id=0, has_side_effects=True),
        )(state, register)
        return pl.pallas_call(
            deliver,
            out_shape=shapes,
            in_specs=[any_space] * 3,
            out_specs=(any_space,) * 3,
            scratch_shapes=[pltpu.VMEM(shape.shape, F32) for shape in shapes] + [pltpu.SemaphoreType.DMA((6,))],
        )(*results)

    return jax.shard_map(local, mesh=mesh, in_specs=(spec, spec), out_specs=(spec,) * 3, check_vma=False)
```

```python
import functools

import jax
import jax.numpy as jnp
from jax import lax
from jax.experimental import pallas as pl
from jax.experimental.pallas import tpu as pltpu
from jax.sharding import PartitionSpec as P

F32 = jnp.float32
CFL_NUMBER = 0.3
SECTION_DECAY = -5.0 / 9.0
SECTION_GAIN = 15.0 / 16.0
NF = 5
LX = 8
LZ = 128
SPARE = (LX + 6) * 8


def weno_pair(a, b, c, d, e):
    e1 = b - a
    e2 = c - b
    e3 = d - c
    e4 = e - d
    d0 = e2 - e1
    d1 = e3 - e2
    d2 = e4 - e3
    g0 = d0 + 2.0 * e2
    g1 = e2 + e3
    g2 = d2 - 2.0 * e3
    third = 13.0 / 3.0
    s0 = (third * d0) * d0 + g0 * g0 + 4e-6
    s1 = (third * d1) * d1 + g1 * g1 + 4e-6
    s2 = (third * d2) * d2 + g2 * g2 + 4e-6
    t0 = s0 * s0
    t1 = s1 * s1
    t2 = s2 * s2
    n0 = t1 * t2
    n1 = 6.0 * (t0 * t2)
    n2 = t0 * t1
    n0_three = 3.0 * n0
    n2_three = 3.0 * n2
    left_up = n0 * (5.0 * e2 - 2.0 * e1) + n1 * (2.0 * e3 + e2) + n2_three * (4.0 * e3 - e4)
    right_up = n2 * (5.0 * e3 - 2.0 * e4) + n1 * (2.0 * e2 + e3) + n0_three * (4.0 * e2 - e1)
    left = c + left_up / (6.0 * (n0 + n1 + n2_three))
    right = c - right_up / (6.0 * (n2 + n1 + n0_three))
    return left, right


def floored(face, lower, upper):
    return (
        jnp.maximum(face[0], 0.5 * jnp.minimum(lower[0], upper[0])),
        face[1],
        face[2],
        face[3],
        jnp.maximum(face[4], 0.5 * jnp.minimum(lower[1], upper[1])),
    )


def hlle(left, right, normal):
    def terms(s):
        rho, u, v, w, p = s
        sound = jnp.sqrt(1.4 * p / rho)
        energy = 2.5 * p + 0.5 * rho * (u * u + v * v + w * w)
        return (rho, rho * u, rho * v, rho * w, energy), s[normal], sound

    ul, nl, cl = terms(left)
    ur, nr, cr = terms(right)
    sm = jnp.minimum(jnp.minimum(nl - cl, nr - cr), 0.0)
    sp = jnp.maximum(jnp.maximum(nl + cl, nr + cr), 0.0)
    inv = 1.0 / (sp - sm)
    spi = sp * inv
    smi = sm * inv
    al = spi * (nl - sm)
    ar = smi * (sp - nr)
    pl_ = spi * left[4]
    pr_ = smi * right[4]
    flux = [al * ul[k] + ar * ur[k] for k in range(NF)]
    flux[normal] = flux[normal] + (pl_ - pr_)
    flux[4] = flux[4] + (pl_ * nl - pr_ * nr)
    return tuple(flux)


def kernel(
    sizes,
    state,
    register,
    o_state,
    o_reg,
    o_coef,
    st,
    rg,
    px,
    py,
    ez,
    ezl,
    ezh,
    sides_x,
    sides_y,
    flux_x,
    flux_y,
    fz,
    sn,
    rn,
    base,
    rate,
    ends,
    turned,
    around,
    sx_hi,
    sx_lo,
    rx_lo,
    rx_hi,
    sz,
    rz,
    fn,
    fy,
    fc,
    coef,
    mx,
    my,
    mz,
    local_sem,
    halo_send,
    halo_recv,
    max_send,
    max_recv,
    lift_send,
    lift_recv,
    known,
):
    nx, ny, nz = sizes
    ix = lax.axis_index("gx")
    iy = lax.axis_index("gy")
    iz = lax.axis_index("gz")

    def turned_by(i, k, n):
        k = k % n
        return i if k == 0 else jnp.where(i >= n - k, i - (n - k), i + k)

    def at(dx=0, dy=0, dz=0):
        return {"gx": turned_by(ix, dx, nx), "gy": turned_by(iy, dy, ny), "gz": turned_by(iz, dz, nz)}

    chips_z, half_y = nx // 2, ny // 2
    upper_half = jnp.where(ix >= chips_z, 1, 0)
    chip_z = ix - upper_half * chips_z
    core = lax.rem(iy, 2)
    chip_y = upper_half * half_y + lax.div(iy, 2)

    def plane_mate(k):
        return {"gx": ix, "gy": iy if k < nz else iy + 1 - 2 * core, "gz": turned_by(iz, k, nz)}

    def column_mate(k):
        y = turned_by(chip_y, k, 2 * half_y)
        half = jnp.where(y >= half_y, 1, 0)
        return {"gx": half * chips_z + chip_z, "gy": (y - half * half_y) * 2 + core, "gz": iz}

    def depth_mate(k):
        return {"gx": upper_half * chips_z + turned_by(chip_z, k, chips_z), "gy": iy, "gz": iz}

    groups = ((plane_mate, 2 * nz), (column_mate, 2 * half_y), (depth_mate, chips_z))

    def far_first(count):
        return sorted(range(1, count), key=lambda k: -min(k, count - k))

    orders = (sorted(range(1, 2 * nz), key=lambda k: -min(k % nz, nz - k % nz)), far_first(2 * half_y), far_first(chips_z))

    barrier = pltpu.get_barrier_semaphore()

    def greet(target):
        pl.semaphore_signal(barrier, inc=1, device_id=target, device_id_type=pl.DeviceIdType.MESH)

    load_state = pltpu.make_async_copy(state, st, local_sem.at[0])
    load_reg = pltpu.make_async_copy(register, rg, local_sem.at[1])
    load_state.start()
    load_reg.start()
    near = ((depth_mate, chips_z), (column_mate, 2 * half_y))
    offsets = [(mate, k) for mate, n in near for k in sorted({2 % n, 1 % n, n - 1, (n - 2) % n} - {0})]
    offsets += [(plane_mate, k) for k in orders[0]]
    for mate, k in offsets:
        greet(mate(k))
    for target in (at(dx=-1), at(dx=1)):
        greet(target)
    for dy in (-1, 0, 1):
        for dz in (-1, 0, 1):
            if (dy, dz) != (0, 0):
                greet(at(dy=dy, dz=dz))
    partners = len(offsets) + 10

    lane = lax.broadcasted_iota(jnp.int32, (8, LZ), 1)
    row = lax.broadcasted_iota(jnp.int32, (8, LZ), 0)
    group = lane // 16
    inner = lane % 16

    load_state.wait()

    def make_primitives(x, top):
        rho = st[0, x]
        inv = 1.0 / rho
        u = st[1, x] * inv
        v = st[2, x] * inv
        w = st[3, x] * inv
        p = 0.4 * (st[4, x] - 0.5 * rho * (u * u + v * v + w * w))
        here = (rho, u, v, w, p)
        rows = pl.ds(pl.multiple_of((x + 3) * 8, 8), 8)
        for k in range(NF):
            px[k, rows, :] = here[k]
        speed = jnp.maximum(jnp.maximum(jnp.abs(u), jnp.abs(v)), jnp.abs(w)) + jnp.sqrt(1.4 * p * inv)
        return jnp.maximum(top, speed)

    zero = jnp.zeros((8, LZ), F32)
    top = lax.fori_loop(0, LX, make_primitives, zero, unroll=4)
    top = jnp.max(jnp.max(top, axis=0, keepdims=True), axis=1, keepdims=True)
    mz[0] = jnp.broadcast_to(top, (1, LZ))

    pl.semaphore_wait(barrier, partners)

    def remote(src, dst, send, recv, target):
        return pltpu.make_async_remote_copy(
            src_ref=src,
            dst_ref=dst,
            send_sem=send,
            recv_sem=recv,
            device_id=target,
            device_id_type=pl.DeviceIdType.MESH,
        )

    bases = (0, groups[0][1], groups[0][1] + groups[1][1])
    slots = (mz, my, mx)

    def max_copy(i, k):
        sem = bases[i] + k
        return remote(slots[i].at[0], slots[i].at[k], max_send.at[sem], max_recv.at[sem], groups[i][0](k))

    def max_start(i):
        for k in orders[i]:
            max_copy(i, k).start()

    def max_wait(i):
        best = slots[i][0]
        for k in reversed(orders[i]):
            max_copy(i, k).wait_recv()
            best = jnp.maximum(best, slots[i][k])
        return best

    def max_sent(i):
        for k in orders[i]:
            max_copy(i, k).wait_send()

    low, high = pl.ds(0, 24), pl.ds(88, 24)
    first, last = pl.ds(24, 24), pl.ds(64, 24)
    halos = [
        remote(ez, ezl, halo_send.at[0], halo_recv.at[0], at(dz=1)),
        remote(ez, ezh, halo_send.at[1], halo_recv.at[1], at(dz=-1)),
        remote(py.at[:, last, :], py.at[:, low, :], halo_send.at[2], halo_recv.at[2], at(dy=1)),
        remote(py.at[:, first, :], py.at[:, high, :], halo_send.at[3], halo_recv.at[3], at(dy=-1)),
        remote(px.at[:, last, :], px.at[:, low, :], halo_send.at[4], halo_recv.at[4], at(dx=1)),
        remote(px.at[:, first, :], px.at[:, high, :], halo_send.at[5], halo_recv.at[5], at(dx=-1)),
    ]
    halos[4].start()
    halos[5].start()
    max_start(0)

    def hand_on(mate, n, sem):
        for k in (2, n - 2):
            pl.semaphore_signal(known.at[sem], inc=1, device_id=mate(k), device_id_type=pl.DeviceIdType.MESH)

    def heard(sem):
        pl.semaphore_wait(known.at[sem], 2)

    far_y, far_z, farther_z = half_y > 2, chips_z > 5, chips_z > 9
    if far_z:
        hand_on(depth_mate, chips_z, 1)
    if far_y:
        hand_on(column_mate, 2 * half_y, 0)

    def turn(y, _):
        rows = pl.ds(pl.multiple_of((y + 3) * 8, 8), 8)
        for k in range(NF):
            py[k, rows, :] = px[k, pl.ds(24 + y, 8, stride=8), :]
        return 0

    lax.fori_loop(0, LX, turn, 0, unroll=4)
    halos[2].start()
    halos[3].start()

    def pack_edges(x, edges):
        rows = pl.ds(pl.multiple_of((x + 3) * 8, 8), 8)
        return tuple(
            jnp.where(group == x, pltpu.roll(px[k, rows, :], 16 * x + 3, 1), edges[k]) for k in range(NF)
        )

    edges = lax.fori_loop(0, LX, pack_edges, (zero,) * NF, unroll=4)
    for k in range(NF):
        ez[k] = edges[k]
    halos[0].start()
    halos[1].start()

    def slot(i):
        return pl.ds(8 * i if isinstance(i, int) else pl.multiple_of(i * 8, 8), 8)

    def plane(v, k, x):
        return (base, rate)[v][k, slot(x), :]

    def lift_copies(v):
        def one(i, src, dst, target):
            return remote(src, dst, lift_send.at[8 * v + i], lift_recv.at[8 * v + i], target)

        to_hi, to_lo = pl.ds(0, 16), pl.ds(16, 24)
        copies = [
            one(0, turned.at[v, :, to_hi, :], around.at[v, :, to_hi, :], at(dy=1)),
            one(1, turned.at[v, :, to_lo, :], around.at[v, :, to_lo, :], at(dy=-1)),
        ]
        for i, (dy, dz) in enumerate(((1, 1), (1, -1), (-1, 1), (-1, -1), (0, 1), (0, -1))):
            copies.append(one(2 + i, sz.at[v], rz.at[v, i], at(dy=dy, dz=dz)))
        return copies

    lifts = [lift_copies(0), lift_copies(1)]
    for v in range(2):
        for k in range(NF):
            around[v, k, pl.ds(40, 32), :] = jnp.zeros((32, LZ), F32)

    def send_lift(v, make):
        source = (base, rate)[v]

        def pack_ends(x, packed):
            values = make(x)
            for k in range(NF):
                source[k, slot(x), :] = values[k]
            return tuple(jnp.where(group == x, pltpu.roll(values[k], 16 * x + 4, 1), packed[k]) for k in range(NF))

        packed = lax.fori_loop(0, LX, pack_ends, (zero,) * NF, unroll=4)
        for k in range(NF):
            sz[v, k] = packed[k]
        for copy in lifts[v][2:]:
            copy.start()
        for k in range(NF):
            for i, y in enumerate((4, 6, 0, 2, 4)):
                turned[v, k, pl.ds(8 * i, 8), :] = source[k, pl.ds(y, 8, stride=8), :]
        lifts[v][0].start()
        lifts[v][1].start()

    from_low = inner < 4

    def receive_lift(v):
        for copy in lifts[v]:
            copy.wait_recv()
        for k in range(NF):
            below = jnp.where(from_low, rz[v, 0, k], rz[v, 1, k])
            above = jnp.where(from_low, rz[v, 2, k], rz[v, 3, k])
            outer = jnp.where(row == 0, pltpu.roll(below, 4, 0), pltpu.roll(below, 3, 0))
            outer = jnp.where(row == 2, pltpu.roll(above, 2, 0), outer)
            outer = jnp.where(row == 3, pltpu.roll(above, 1, 0), outer)
            ends[v, k, pl.ds(0, 8), :] = jnp.where(from_low, rz[v, 4, k], rz[v, 5, k])
            ends[v, k, pl.ds(8, 8), :] = jnp.where(row == 4, above, outer)


    def cell_faces(padded, sides, j):
        for k in range(NF):
            a, b, c, d, e = (padded[k, slot(j + i), :] for i in range(5))
            sides[0, k, slot(j), :], sides[1, k, slot(j), :] = weno_pair(a, b, c, d, e)

    def face_flux(padded, sides, flux, normal, f):
        lower = padded[0, slot(f + 2), :], padded[4, slot(f + 2), :]
        upper = padded[0, slot(f + 3), :], padded[4, slot(f + 3), :]
        left = floored([sides[0, k, slot(f), :] for k in range(NF)], lower, upper)
        right = floored([sides[1, k, slot(f + 1), :] for k in range(NF)], lower, upper)
        for k, value in enumerate(hlle(left, right, normal)):
            flux[k, slot(f), :] = value

    def sweep_inner(padded, sides, flux, normal):
        def cells(i, _):
            cell_faces(padded, sides, 3 + i)
            cell_faces(padded, sides, 5 + i)
            return 0

        def faces(i, _):
            face_flux(padded, sides, flux, normal, 3 + i)
            return 0

        lax.fori_loop(0, 2, cells, 0)
        lax.fori_loop(0, 3, faces, 0)

    def sweep_outer(padded, sides, flux, normal):
        def cells(i, _):
            cell_faces(padded, sides, i)
            cell_faces(padded, sides, 7 + i)
            return 0

        def faces(i, _):
            face_flux(padded, sides, flux, normal, i)
            face_flux(padded, sides, flux, normal, 6 + i)
            return 0

        lax.fori_loop(0, 3, cells, 0)
        lax.fori_loop(0, 3, faces, 0)

    if far_z:
        heard(1)
    if farther_z:
        hand_on(depth_mate, chips_z, 2)
    my[0] = max_wait(0)
    if far_y:
        heard(0)
    max_start(1)

    load_reg.wait()

    def make_base(x):
        return [st[k, x] + (SECTION_GAIN * SECTION_DECAY) * rg[k, x] for k in range(NF)]

    send_lift(0, make_base)
    sweep_inner(px, sides_x, flux_x, 1)
    sweep_inner(py, sides_y, flux_y, 2)
    halos[0].wait_recv()
    halos[1].wait_recv()
    for k in range(NF):
        lower = jnp.where(inner < 3, ezl[k], ez[k])
        upper = pltpu.roll(jnp.where(inner < 3, ez[k], ezh[k]), 8, 1)
        px[k, pl.ds(SPARE, 8), :] = jnp.where(inner < 8, lower, upper)

    def z_faces(x, _):
        rows = pl.ds(pl.multiple_of((x + 3 + 3 * (x // LX)) * 8, 8), 8)
        left, right, cell, nxt = [], [], [], []
        for k in range(NF):
            c = px[k, rows, :]
            outside = pltpu.roll(jnp.where(inner < 3, ezl[k], ezh[k]), lax.rem(253 - 16 * x, LZ), 1)
            a = pltpu.roll(jnp.where(lane >= LZ - 2, outside, c), 2, 1)
            b = pltpu.roll(jnp.where(lane >= LZ - 1, outside, c), 1, 1)
            d = pltpu.roll(jnp.where(lane < 1, outside, c), LZ - 1, 1)
            e = pltpu.roll(jnp.where(lane < 2, outside, c), LZ - 2, 1)
            lk, rk = weno_pair(a, b, c, d, e)
            left.append(lk)
            right.append(pltpu.roll(rk, LZ - 1, 1))
            cell.append(c)
            nxt.append(d)
        sides = (cell[0], cell[4]), (nxt[0], nxt[4])
        flux = hlle(floored(left, *sides), floored(right, *sides), 3)
        out = pl.ds(pl.multiple_of(x * 8, 8), 8)
        for k in range(NF):
            fz[k, out, :] = flux[k]
        return 0

    lax.fori_loop(0, LX + 1, z_faces, 0)
    for k in range(NF):
        tail = fz[k, pl.ds(64, 8), :]
        fz[k, pl.ds(64, 8), :] = jnp.where(inner == 11, pltpu.roll(tail, 9, 1), tail)

    halos[2].wait_recv()
    halos[3].wait_recv()
    sweep_outer(py, sides_y, flux_y, 2)

    def make_rate(x, _):
        for k in range(NF):
            faces = fz[k, slot(x), :]
            tips = pltpu.roll(fz[k, pl.ds(64, 8), :], 117 - 16 * x, 1)
            upper = jnp.where(lane == LZ - 1, tips, faces)
            lower = jnp.where(lane == 0, tips, pltpu.roll(faces, 1, 1))
            upper_y = flux_y[k, pl.ds(8 + x, 8, stride=8), :]
            lower_y = flux_y[k, pl.ds(x, 8, stride=8), :]
            rate[k, slot(x), :] = (lower - upper) + (lower_y - upper_y)
        return 0

    lax.fori_loop(0, LX, make_rate, 0, unroll=4)
    halos[4].wait_recv()
    halos[5].wait_recv()
    sweep_outer(px, sides_x, flux_x, 1)

    def finish_rate(x):
        return [rate[k, slot(x), :] + (flux_x[k, slot(x), :] - flux_x[k, slot(x + 1), :]) for k in range(NF)]

    send_lift(1, finish_rate)
    mx[0] = max_wait(1)
    if farther_z:
        heard(2)
    max_start(2)
    receive_lift(0)
    receive_lift(1)

    fastest = max_wait(2)
    step = jnp.broadcast_to(CFL_NUMBER / fastest, (8, LZ))
    gain = SECTION_GAIN * step

    def pressure(new):
        square = new[1] * new[1] + new[2] * new[2] + new[3] * new[3]
        return 0.4 * (new[4] - 0.5 * square / new[0])

    for j in range(2):
        new = [ends[0, k, slot(j), :] + gain * ends[1, k, slot(j), :] for k in range(NF)]
        fc[0, slot(j), :] = pressure(new)
        fc[1, slot(j), :] = new[0]

    def after(x):
        new = [plane(0, k, x) + gain * plane(1, k, x) for k in range(NF)]
        return pressure(new), new[0]

    def after_around(x):
        rows = pl.ds(x, 8, stride=8)
        new = [around[0, k, rows, :] + gain * around[1, k, rows, :] for k in range(NF)]
        return pressure(new), new[0]

    odd_lane = lane % 2 == 1
    mid_lane = lane % 4 == 2
    odd_row = row % 2 == 1
    mid_row = row % 4 == 2

    def predicted(down1, up1, down3, up3):
        return (9.0 * (down1 + up1) - (down3 + up3)) * 0.0625

    def fine_z(c, ends):
        up1 = pltpu.roll(jnp.where(lane < 1, ends, c), LZ - 1, 1)
        up3 = pltpu.roll(jnp.where(lane < 3, ends, c), LZ - 3, 1)
        down1 = pltpu.roll(c, 1, 1)
        down3 = pltpu.roll(jnp.where(lane >= LZ - 3, ends, c), 3, 1)
        return jnp.where(odd_lane, c - predicted(down1, up1, down3, up3), c)

    def coarse_z(c, ends):
        up2 = pltpu.roll(jnp.where(lane < 2, ends, c), LZ - 2, 1)
        up6 = pltpu.roll(jnp.where(lane < 6, ends, c), LZ - 6, 1)
        down2 = pltpu.roll(c, 2, 1)
        down6 = pltpu.roll(jnp.where(lane >= LZ - 6, ends, c), 6, 1)
        return jnp.where(mid_lane, c - predicted(down2, up2, down6, up6), c)

    def fine_y(c, outer):
        down1 = pltpu.roll(c, 1, 0)
        down3 = jnp.where(row == 1, outer, pltpu.roll(c, 3, 0))
        up1 = jnp.where(row == 7, pltpu.roll(outer, 5, 0), pltpu.roll(c, 7, 0))
        up3 = jnp.where(row == 7, pltpu.roll(outer, 4, 0), pltpu.roll(c, 5, 0))
        up3 = jnp.where(row == 5, pltpu.roll(outer, 3, 0), up3)
        return jnp.where(odd_row, c - predicted(down1, up1, down3, up3), c)

    def coarse_y(c, outer):
        down2 = pltpu.roll(c, 2, 0)
        further = pltpu.roll(c, 6, 0)
        beyond = pltpu.roll(outer, 2, 0)
        up2 = jnp.where(row == 6, pltpu.roll(outer, 4, 0), further)
        down6 = jnp.where(row == 2, beyond, further)
        up6 = jnp.where(row == 2, outer, beyond)
        return jnp.where(mid_row, c - predicted(down2, up2, down6, up6), c)

    def lift_zy(x, out, along_z, along_y):
        cells, outer = after(x), after_around(x)
        for f in range(2):
            tips = pltpu.roll(fc[f, slot(0), :], (252 - 16 * x) % LZ, 1)
            tips_outer = pltpu.roll(fc[f, slot(1), :], (252 - 16 * x) % LZ, 1)
            out[f, slot(x), :] = along_y(along_z(cells[f], tips), along_z(outer[f], tips_outer))

    def lift_fine(x):
        lift_zy(x, fn, fine_z, fine_y)

    def lift_coarse(x):
        lift_zy(x, fy, coarse_z, coarse_y)

    to_high = remote(sx_hi, rx_lo, lift_send.at[16], lift_recv.at[16], at(dx=1))
    to_low = remote(sx_lo, rx_hi, lift_send.at[17], lift_recv.at[17], at(dx=-1))
    lift_fine(6)
    lift_coarse(4)
    for f in range(2):
        sx_hi[f, slot(0), :] = fn[f, slot(6), :]
        sx_hi[f, slot(1), :] = fy[f, slot(4), :]
    to_high.start()
    lift_fine(0)
    lift_fine(2)
    lift_coarse(0)
    for f in range(2):
        sx_lo[f, slot(0), :] = fn[f, slot(0), :]
        sx_lo[f, slot(1), :] = fn[f, slot(2), :]
        sx_lo[f, slot(2), :] = jnp.where(odd_row, pltpu.roll(fy[f, slot(4), :], 1, 0), fy[f, slot(0), :])
    to_low.start()

    def update(x, _):
        for k in range(NF):
            r = SECTION_DECAY * rg[k, x] + step * plane(1, k, x)
            rn[k, x] = r
            sn[k, x] = st[k, x] + SECTION_GAIN * r
        return 0

    lax.fori_loop(0, LX, update, 0, unroll=4)
    store_state = pltpu.make_async_copy(sn, o_state, local_sem.at[2])
    store_reg = pltpu.make_async_copy(rn, o_reg, local_sem.at[3])
    store_state.start()
    store_reg.start()

    for x in (4, 1, 3, 5, 7):
        lift_fine(x)
    for x in (2, 6):
        lift_coarse(x)
    for copy in halos + lifts[0] + lifts[1]:
        copy.wait_send()
    for i in range(3):
        max_sent(i)

    to_high.wait_recv()
    to_low.wait_recv()
    even = jnp.logical_and(row % 2 == 0, lane % 2 == 0)
    for f in range(2):
        fine = {x: fn[f, slot(x), :] for x in range(LX)}
        fine[-2], fine[8], fine[10] = rx_lo[f, slot(0), :], rx_hi[f, slot(0), :], rx_hi[f, slot(1), :]
        coarse = {x: fy[f, slot(x), :] for x in (0, 2, 4, 6)}
        mixed = rx_hi[f, slot(2), :]
        coarse[-4], coarse[8], coarse[12] = rx_lo[f, slot(1), :], mixed, pltpu.roll(mixed, 7, 0)
        for x in range(LX):
            if x % 2 == 1:
                coef[f, x] = fine[x] - predicted(fine[x - 1], fine[x + 1], fine[x - 3], fine[x + 3])
                continue
            value = coarse[x]
            if x % 4 == 2:
                value = value - predicted(coarse[x - 2], coarse[x + 2], coarse[x - 6], coarse[x + 6])
            coef[f, x] = jnp.where(even, value, fine[x])
    store_coef = pltpu.make_async_copy(coef, o_coef, local_sem.at[4])
    store_coef.start()

    to_high.wait_send()
    to_low.wait_send()
    store_state.wait()
    store_reg.wait()
    store_coef.wait()


def deliver(*refs):
    sources, targets, stages, sems = refs[:3], refs[3:6], refs[6:9], refs[9]
    loads = [pltpu.make_async_copy(sources[i], stages[i], sems.at[i]) for i in range(3)]
    stores = [pltpu.make_async_copy(stages[i], targets[i], sems.at[3 + i]) for i in range(3)]
    for load in loads:
        load.start()
    for load, store in zip(loads, stores):
        load.wait()
        store.start()
    for store in stores:
        store.wait()


def solution(mesh):
    sizes = (mesh.shape["gx"], mesh.shape["gy"], mesh.shape["gz"])
    spec = P(None, "gx", "gy", "gz")
    any_space = pl.BlockSpec(memory_space=pl.ANY)

    def vmem(*shape):
        return pltpu.VMEM(shape, F32)

    plane = (8, LZ)
    total = sizes[0] // 2 + sizes[1] + 2 * sizes[2]
    scratch = [
        vmem(NF, LX, *plane),
        vmem(NF, LX, *plane),
        vmem(NF, SPARE + 8, LZ),
        vmem(NF, SPARE, LZ),
        vmem(NF, *plane),
        vmem(NF, *plane),
        vmem(NF, *plane),
        vmem(2, NF, (LX + 2) * 8, LZ),
        vmem(2, NF, (LX + 2) * 8, LZ),
        vmem(NF, (LX + 1) * 8, LZ),
        vmem(NF, (LX + 2) * 8, LZ),
        vmem(NF, (LX + 1) * 8, LZ),
        vmem(NF, LX, *plane),
        vmem(NF, LX, *plane),
        vmem(NF, (LX + 1) * 8, LZ),
        vmem(NF, (LX + 1) * 8, LZ),
        vmem(2, NF, 16, LZ),
        vmem(2, NF, 40, LZ),
        vmem(2, NF, 72, LZ),
        vmem(2, 16, LZ),
        vmem(2, 24, LZ),
        vmem(2, 16, LZ),
        vmem(2, 24, LZ),
        vmem(2, NF, *plane),
        vmem(2, 6, NF, *plane),
        vmem(2, 64, LZ),
        vmem(2, 64, LZ),
        vmem(2, 16, LZ),
        vmem(2, LX, *plane),
        vmem(sizes[0] // 2, 1, LZ),
        vmem(sizes[1], 1, LZ),
        vmem(2 * sizes[2], 1, LZ),
        pltpu.SemaphoreType.DMA((5,)),
        pltpu.SemaphoreType.DMA((6,)),
        pltpu.SemaphoreType.DMA((6,)),
        pltpu.SemaphoreType.DMA((total,)),
        pltpu.SemaphoreType.DMA((total,)),
        pltpu.SemaphoreType.DMA((18,)),
        pltpu.SemaphoreType.DMA((18,)),
        pltpu.SemaphoreType.REGULAR((3,)),
    ]

    def local(state, register):
        block = jax.ShapeDtypeStruct(state.shape, F32)
        shapes = (block, block, jax.ShapeDtypeStruct((2,) + state.shape[1:], F32))
        results = pl.pallas_call(
            functools.partial(kernel, sizes),
            out_shape=shapes,
            in_specs=[any_space] * 2,
            out_specs=(any_space,) * 3,
            scratch_shapes=scratch,
            compiler_params=pltpu.CompilerParams(collective_id=0, has_side_effects=True),
        )(state, register)
        return pl.pallas_call(
            deliver,
            out_shape=shapes,
            in_specs=[any_space] * 3,
            out_specs=(any_space,) * 3,
            scratch_shapes=[pltpu.VMEM(shape.shape, F32) for shape in shapes] + [pltpu.SemaphoreType.DMA((6,))],
        )(*results)

    return jax.shard_map(local, mesh=mesh, in_specs=(spec, spec), out_specs=(spec,) * 3, check_vma=False)
```

```python
import functools

import jax
import jax.numpy as jnp
from jax import lax
from jax.experimental import pallas as pl
from jax.experimental.pallas import tpu as pltpu
from jax.sharding import PartitionSpec as P

F32 = jnp.float32
CFL_NUMBER = 0.3
SECTION_DECAY = -5.0 / 9.0
SECTION_GAIN = 15.0 / 16.0
NF = 5
LX = 8
LZ = 128
SPARE = (LX + 6) * 8


def weno_pair(a, b, c, d, e):
    e1 = b - a
    e2 = c - b
    e3 = d - c
    e4 = e - d
    d0 = e2 - e1
    d1 = e3 - e2
    d2 = e4 - e3
    g0 = d0 + 2.0 * e2
    g1 = e2 + e3
    g2 = d2 - 2.0 * e3
    third = 13.0 / 3.0
    s0 = (third * d0) * d0 + g0 * g0 + 4e-6
    s1 = (third * d1) * d1 + g1 * g1 + 4e-6
    s2 = (third * d2) * d2 + g2 * g2 + 4e-6
    t0 = s0 * s0
    t1 = s1 * s1
    t2 = s2 * s2
    n0 = t1 * t2
    n1 = 6.0 * (t0 * t2)
    n2 = t0 * t1
    n0_three = 3.0 * n0
    n2_three = 3.0 * n2
    left_up = n0 * (5.0 * e2 - 2.0 * e1) + n1 * (2.0 * e3 + e2) + n2_three * (4.0 * e3 - e4)
    right_up = n2 * (5.0 * e3 - 2.0 * e4) + n1 * (2.0 * e2 + e3) + n0_three * (4.0 * e2 - e1)
    left = c + left_up / (6.0 * (n0 + n1 + n2_three))
    right = c - right_up / (6.0 * (n2 + n1 + n0_three))
    return left, right


def floored(face, lower, upper):
    return (
        jnp.maximum(face[0], 0.5 * jnp.minimum(lower[0], upper[0])),
        face[1],
        face[2],
        face[3],
        jnp.maximum(face[4], 0.5 * jnp.minimum(lower[1], upper[1])),
    )


def hlle(left, right, normal):
    def terms(s):
        rho, u, v, w, p = s
        sound = jnp.sqrt(1.4 * p / rho)
        energy = 2.5 * p + 0.5 * rho * (u * u + v * v + w * w)
        return (rho, rho * u, rho * v, rho * w, energy), s[normal], sound

    ul, nl, cl = terms(left)
    ur, nr, cr = terms(right)
    sm = jnp.minimum(jnp.minimum(nl - cl, nr - cr), 0.0)
    sp = jnp.maximum(jnp.maximum(nl + cl, nr + cr), 0.0)
    inv = 1.0 / (sp - sm)
    spi = sp * inv
    smi = sm * inv
    al = spi * (nl - sm)
    ar = smi * (sp - nr)
    pl_ = spi * left[4]
    pr_ = smi * right[4]
    flux = [al * ul[k] + ar * ur[k] for k in range(NF)]
    flux[normal] = flux[normal] + (pl_ - pr_)
    flux[4] = flux[4] + (pl_ * nl - pr_ * nr)
    return tuple(flux)


def kernel(
    sizes,
    state,
    register,
    o_state,
    o_reg,
    o_coef,
    st,
    rg,
    px,
    py,
    ez,
    ezl,
    ezh,
    sides_x,
    sides_y,
    flux_x,
    flux_y,
    fz,
    sn,
    rn,
    base,
    rate,
    ends,
    turned,
    around,
    sx_hi,
    sx_lo,
    rx_lo,
    rx_hi,
    sz,
    rz,
    fn,
    fy,
    fc,
    coef,
    mx,
    my,
    mz,
    local_sem,
    halo_send,
    halo_recv,
    max_send,
    max_recv,
    lift_send,
    lift_recv,
    known,
):
    nx, ny, nz = sizes
    ix = lax.axis_index("gx")
    iy = lax.axis_index("gy")
    iz = lax.axis_index("gz")

    def turned_by(i, k, n):
        k = k % n
        return i if k == 0 else jnp.where(i >= n - k, i - (n - k), i + k)

    def at(dx=0, dy=0, dz=0):
        return {"gx": turned_by(ix, dx, nx), "gy": turned_by(iy, dy, ny), "gz": turned_by(iz, dz, nz)}

    chips_z, half_y = nx // 2, ny // 2
    upper_half = jnp.where(ix >= chips_z, 1, 0)
    chip_z = ix - upper_half * chips_z
    core = lax.rem(iy, 2)
    chip_y = upper_half * half_y + lax.div(iy, 2)

    def plane_mate(k):
        return {"gx": ix, "gy": iy if k < nz else iy + 1 - 2 * core, "gz": turned_by(iz, k, nz)}

    def column_mate(k):
        y = turned_by(chip_y, k, 2 * half_y)
        half = jnp.where(y >= half_y, 1, 0)
        return {"gx": half * chips_z + chip_z, "gy": (y - half * half_y) * 2 + core, "gz": iz}

    def depth_mate(k):
        return {"gx": upper_half * chips_z + turned_by(chip_z, k, chips_z), "gy": iy, "gz": iz}

    groups = ((plane_mate, 2 * nz), (column_mate, 2 * half_y), (depth_mate, chips_z))

    def far_first(count):
        return sorted(range(1, count), key=lambda k: -min(k, count - k))

    orders = (sorted(range(1, 2 * nz), key=lambda k: -min(k % nz, nz - k % nz)), far_first(2 * half_y), far_first(chips_z))

    barrier = pltpu.get_barrier_semaphore()

    def greet(target):
        pl.semaphore_signal(barrier, inc=1, device_id=target, device_id_type=pl.DeviceIdType.MESH)

    load_state = pltpu.make_async_copy(state, st, local_sem.at[0])
    load_reg = pltpu.make_async_copy(register, rg, local_sem.at[1])
    load_state.start()
    load_reg.start()
    near = ((depth_mate, chips_z), (column_mate, 2 * half_y))
    offsets = [(mate, k) for mate, n in near for k in sorted({2 % n, 1 % n, n - 1, (n - 2) % n} - {0})]
    offsets += [(plane_mate, k) for k in orders[0]]
    for mate, k in offsets:
        greet(mate(k))
    for target in (at(dx=-1), at(dx=1)):
        greet(target)
    for dy in (-1, 0, 1):
        for dz in (-1, 0, 1):
            if (dy, dz) != (0, 0):
                greet(at(dy=dy, dz=dz))
    partners = len(offsets) + 10

    lane = lax.broadcasted_iota(jnp.int32, (8, LZ), 1)
    row = lax.broadcasted_iota(jnp.int32, (8, LZ), 0)
    group = lane // 16
    inner = lane % 16

    load_state.wait()

    def make_primitives(x, top):
        rho = st[0, x]
        inv = 1.0 / rho
        u = st[1, x] * inv
        v = st[2, x] * inv
        w = st[3, x] * inv
        p = 0.4 * (st[4, x] - 0.5 * rho * (u * u + v * v + w * w))
        here = (rho, u, v, w, p)
        rows = pl.ds(pl.multiple_of((x + 3) * 8, 8), 8)
        for k in range(NF):
            px[k, rows, :] = here[k]
        speed = jnp.maximum(jnp.maximum(jnp.abs(u), jnp.abs(v)), jnp.abs(w)) + jnp.sqrt(1.4 * p * inv)
        return jnp.maximum(top, speed)

    zero = jnp.zeros((8, LZ), F32)
    top = lax.fori_loop(0, LX, make_primitives, zero, unroll=4)
    top = jnp.max(jnp.max(top, axis=0, keepdims=True), axis=1, keepdims=True)
    mz[0] = jnp.broadcast_to(top, (1, LZ))

    pl.semaphore_wait(barrier, partners)

    def remote(src, dst, send, recv, target):
        return pltpu.make_async_remote_copy(
            src_ref=src,
            dst_ref=dst,
            send_sem=send,
            recv_sem=recv,
            device_id=target,
            device_id_type=pl.DeviceIdType.MESH,
        )

    bases = (0, groups[0][1], groups[0][1] + groups[1][1])
    slots = (mz, my, mx)

    def max_copy(i, k):
        sem = bases[i] + k
        return remote(slots[i].at[0], slots[i].at[k], max_send.at[sem], max_recv.at[sem], groups[i][0](k))

    def max_start(i):
        for k in orders[i]:
            max_copy(i, k).start()

    def max_wait(i):
        best = slots[i][0]
        for k in reversed(orders[i]):
            max_copy(i, k).wait_recv()
            best = jnp.maximum(best, slots[i][k])
        return best

    def max_sent(i):
        for k in orders[i]:
            max_copy(i, k).wait_send()

    low, high = pl.ds(0, 24), pl.ds(88, 24)
    first, last = pl.ds(24, 24), pl.ds(64, 24)
    halos = [
        remote(ez, ezl, halo_send.at[0], halo_recv.at[0], at(dz=1)),
        remote(ez, ezh, halo_send.at[1], halo_recv.at[1], at(dz=-1)),
        remote(py.at[:, last, :], py.at[:, low, :], halo_send.at[2], halo_recv.at[2], at(dy=1)),
        remote(py.at[:, first, :], py.at[:, high, :], halo_send.at[3], halo_recv.at[3], at(dy=-1)),
        remote(px.at[:, last, :], px.at[:, low, :], halo_send.at[4], halo_recv.at[4], at(dx=1)),
        remote(px.at[:, first, :], px.at[:, high, :], halo_send.at[5], halo_recv.at[5], at(dx=-1)),
    ]
    halos[4].start()
    halos[5].start()
    max_start(0)

    def hand_on(mate, n, sem):
        for k in (2, n - 2):
            pl.semaphore_signal(known.at[sem], inc=1, device_id=mate(k), device_id_type=pl.DeviceIdType.MESH)

    def heard(sem):
        pl.semaphore_wait(known.at[sem], 2)

    far_y, far_z, farther_z = half_y > 2, chips_z > 5, chips_z > 9
    if far_z:
        hand_on(depth_mate, chips_z, 1)
    if far_y:
        hand_on(column_mate, 2 * half_y, 0)

    def turn(y, _):
        rows = pl.ds(pl.multiple_of((y + 3) * 8, 8), 8)
        for k in range(NF):
            py[k, rows, :] = px[k, pl.ds(24 + y, 8, stride=8), :]
        return 0

    lax.fori_loop(0, LX, turn, 0, unroll=4)
    halos[2].start()
    halos[3].start()

    def pack_edges(x, edges):
        rows = pl.ds(pl.multiple_of((x + 3) * 8, 8), 8)
        return tuple(
            jnp.where(group == x, pltpu.roll(px[k, rows, :], 16 * x + 3, 1), edges[k]) for k in range(NF)
        )

    edges = lax.fori_loop(0, LX, pack_edges, (zero,) * NF, unroll=4)
    for k in range(NF):
        ez[k] = edges[k]
    halos[0].start()
    halos[1].start()

    def slot(i):
        return pl.ds(8 * i if isinstance(i, int) else pl.multiple_of(i * 8, 8), 8)

    def plane(v, k, x):
        return (base, rate)[v][k, slot(x), :]

    def lift_copies(v):
        def one(i, src, dst, target):
            return remote(src, dst, lift_send.at[8 * v + i], lift_recv.at[8 * v + i], target)

        to_hi, to_lo = pl.ds(0, 16), pl.ds(16, 24)
        copies = [
            one(0, turned.at[v, :, to_hi, :], around.at[v, :, to_hi, :], at(dy=1)),
            one(1, turned.at[v, :, to_lo, :], around.at[v, :, to_lo, :], at(dy=-1)),
        ]
        for i, (dy, dz) in enumerate(((1, 1), (1, -1), (-1, 1), (-1, -1), (0, 1), (0, -1))):
            copies.append(one(2 + i, sz.at[v], rz.at[v, i], at(dy=dy, dz=dz)))
        return copies

    lifts = [lift_copies(0), lift_copies(1)]
    for v in range(2):
        for k in range(NF):
            around[v, k, pl.ds(40, 32), :] = jnp.zeros((32, LZ), F32)

    def send_lift(v, make):
        source = (base, rate)[v]

        def pack_ends(x, packed):
            values = make(x)
            for k in range(NF):
                source[k, slot(x), :] = values[k]
            return tuple(jnp.where(group == x, pltpu.roll(values[k], 16 * x + 4, 1), packed[k]) for k in range(NF))

        packed = lax.fori_loop(0, LX, pack_ends, (zero,) * NF, unroll=4)
        for k in range(NF):
            sz[v, k] = packed[k]
        for copy in lifts[v][2:]:
            copy.start()
        for k in range(NF):
            for i, y in enumerate((4, 6, 0, 2, 4)):
                turned[v, k, pl.ds(8 * i, 8), :] = source[k, pl.ds(y, 8, stride=8), :]
        lifts[v][0].start()
        lifts[v][1].start()

    from_low = inner < 4

    def receive_lift(v):
        for copy in lifts[v]:
            copy.wait_recv()
        for k in range(NF):
            below = jnp.where(from_low, rz[v, 0, k], rz[v, 1, k])
            above = jnp.where(from_low, rz[v, 2, k], rz[v, 3, k])
            outer = jnp.where(row == 0, pltpu.roll(below, 4, 0), pltpu.roll(below, 3, 0))
            outer = jnp.where(row == 2, pltpu.roll(above, 2, 0), outer)
            outer = jnp.where(row == 3, pltpu.roll(above, 1, 0), outer)
            ends[v, k, pl.ds(0, 8), :] = jnp.where(from_low, rz[v, 4, k], rz[v, 5, k])
            ends[v, k, pl.ds(8, 8), :] = jnp.where(row == 4, above, outer)


    def cell_faces(padded, sides, j):
        for k in range(NF):
            a, b, c, d, e = (padded[k, slot(j + i), :] for i in range(5))
            sides[0, k, slot(j), :], sides[1, k, slot(j), :] = weno_pair(a, b, c, d, e)

    def face_flux(padded, sides, flux, normal, f):
        lower = padded[0, slot(f + 2), :], padded[4, slot(f + 2), :]
        upper = padded[0, slot(f + 3), :], padded[4, slot(f + 3), :]
        left = floored([sides[0, k, slot(f), :] for k in range(NF)], lower, upper)
        right = floored([sides[1, k, slot(f + 1), :] for k in range(NF)], lower, upper)
        for k, value in enumerate(hlle(left, right, normal)):
            flux[k, slot(f), :] = value

    def sweep_inner(padded, sides, flux, normal):
        def cells(i, _):
            cell_faces(padded, sides, 3 + i)
            cell_faces(padded, sides, 5 + i)
            return 0

        def faces(i, _):
            face_flux(padded, sides, flux, normal, 3 + i)
            return 0

        lax.fori_loop(0, 2, cells, 0)
        lax.fori_loop(0, 3, faces, 0)

    def sweep_outer(padded, sides, flux, normal):
        def cells(i, _):
            cell_faces(padded, sides, i)
            cell_faces(padded, sides, 7 + i)
            return 0

        def faces(i, _):
            face_flux(padded, sides, flux, normal, i)
            face_flux(padded, sides, flux, normal, 6 + i)
            return 0

        lax.fori_loop(0, 3, cells, 0, unroll=True)
        lax.fori_loop(0, 3, faces, 0, unroll=True)

    sweep_inner(px, sides_x, flux_x, 1)
    sweep_inner(py, sides_y, flux_y, 2)
    if far_z:
        heard(1)
    if farther_z:
        hand_on(depth_mate, chips_z, 2)
    my[0] = max_wait(0)
    if far_y:
        heard(0)
    max_start(1)

    load_reg.wait()

    def make_base(x):
        return [st[k, x] + (SECTION_GAIN * SECTION_DECAY) * rg[k, x] for k in range(NF)]

    send_lift(0, make_base)
    halos[0].wait_recv()
    halos[1].wait_recv()
    for k in range(NF):
        lower = jnp.where(inner < 3, ezl[k], ez[k])
        upper = pltpu.roll(jnp.where(inner < 3, ez[k], ezh[k]), 8, 1)
        px[k, pl.ds(SPARE, 8), :] = jnp.where(inner < 8, lower, upper)

    def z_faces(x, _):
        rows = pl.ds(pl.multiple_of((x + 3 + 3 * (x // LX)) * 8, 8), 8)
        left, right, cell, nxt = [], [], [], []
        for k in range(NF):
            c = px[k, rows, :]
            outside = pltpu.roll(jnp.where(inner < 3, ezl[k], ezh[k]), lax.rem(253 - 16 * x, LZ), 1)
            a = pltpu.roll(jnp.where(lane >= LZ - 2, outside, c), 2, 1)
            b = pltpu.roll(jnp.where(lane >= LZ - 1, outside, c), 1, 1)
            d = pltpu.roll(jnp.where(lane < 1, outside, c), LZ - 1, 1)
            e = pltpu.roll(jnp.where(lane < 2, outside, c), LZ - 2, 1)
            lk, rk = weno_pair(a, b, c, d, e)
            left.append(lk)
            right.append(pltpu.roll(rk, LZ - 1, 1))
            cell.append(c)
            nxt.append(d)
        sides = (cell[0], cell[4]), (nxt[0], nxt[4])
        flux = hlle(floored(left, *sides), floored(right, *sides), 3)
        out = pl.ds(pl.multiple_of(x * 8, 8), 8)
        for k in range(NF):
            fz[k, out, :] = flux[k]
        return 0

    lax.fori_loop(0, LX + 1, z_faces, 0)
    for k in range(NF):
        tail = fz[k, pl.ds(64, 8), :]
        fz[k, pl.ds(64, 8), :] = jnp.where(inner == 11, pltpu.roll(tail, 9, 1), tail)

    halos[2].wait_recv()
    halos[3].wait_recv()
    sweep_outer(py, sides_y, flux_y, 2)

    def make_rate(x, _):
        for k in range(NF):
            faces = fz[k, slot(x), :]
            tips = pltpu.roll(fz[k, pl.ds(64, 8), :], 117 - 16 * x, 1)
            upper = jnp.where(lane == LZ - 1, tips, faces)
            lower = jnp.where(lane == 0, tips, pltpu.roll(faces, 1, 1))
            upper_y = flux_y[k, pl.ds(8 + x, 8, stride=8), :]
            lower_y = flux_y[k, pl.ds(x, 8, stride=8), :]
            rate[k, slot(x), :] = (lower - upper) + (lower_y - upper_y)
        return 0

    lax.fori_loop(0, LX, make_rate, 0, unroll=4)
    halos[4].wait_recv()
    halos[5].wait_recv()
    sweep_outer(px, sides_x, flux_x, 1)

    def finish_rate(x):
        return [rate[k, slot(x), :] + (flux_x[k, slot(x), :] - flux_x[k, slot(x + 1), :]) for k in range(NF)]

    send_lift(1, finish_rate)
    mx[0] = max_wait(1)
    if farther_z:
        heard(2)
    max_start(2)
    receive_lift(0)
    receive_lift(1)

    fastest = max_wait(2)
    step = jnp.broadcast_to(CFL_NUMBER / fastest, (8, LZ))
    gain = SECTION_GAIN * step

    def pressure(new):
        square = new[1] * new[1] + new[2] * new[2] + new[3] * new[3]
        return 0.4 * (new[4] - 0.5 * square / new[0])

    for j in range(2):
        new = [ends[0, k, slot(j), :] + gain * ends[1, k, slot(j), :] for k in range(NF)]
        fc[0, slot(j), :] = pressure(new)
        fc[1, slot(j), :] = new[0]

    def after(x):
        new = [plane(0, k, x) + gain * plane(1, k, x) for k in range(NF)]
        return pressure(new), new[0]

    def after_around(x):
        rows = pl.ds(x, 8, stride=8)
        new = [around[0, k, rows, :] + gain * around[1, k, rows, :] for k in range(NF)]
        return pressure(new), new[0]

    odd_lane = lane % 2 == 1
    mid_lane = lane % 4 == 2
    odd_row = row % 2 == 1
    mid_row = row % 4 == 2

    def predicted(down1, up1, down3, up3):
        return (9.0 * (down1 + up1) - (down3 + up3)) * 0.0625

    def fine_z(c, ends):
        up1 = pltpu.roll(jnp.where(lane < 1, ends, c), LZ - 1, 1)
        up3 = pltpu.roll(jnp.where(lane < 3, ends, c), LZ - 3, 1)
        down1 = pltpu.roll(c, 1, 1)
        down3 = pltpu.roll(jnp.where(lane >= LZ - 3, ends, c), 3, 1)
        return jnp.where(odd_lane, c - predicted(down1, up1, down3, up3), c)

    def coarse_z(c, ends):
        up2 = pltpu.roll(jnp.where(lane < 2, ends, c), LZ - 2, 1)
        up6 = pltpu.roll(jnp.where(lane < 6, ends, c), LZ - 6, 1)
        down2 = pltpu.roll(c, 2, 1)
        down6 = pltpu.roll(jnp.where(lane >= LZ - 6, ends, c), 6, 1)
        return jnp.where(mid_lane, c - predicted(down2, up2, down6, up6), c)

    def fine_y(c, outer):
        down1 = pltpu.roll(c, 1, 0)
        down3 = jnp.where(row == 1, outer, pltpu.roll(c, 3, 0))
        up1 = jnp.where(row == 7, pltpu.roll(outer, 5, 0), pltpu.roll(c, 7, 0))
        up3 = jnp.where(row == 7, pltpu.roll(outer, 4, 0), pltpu.roll(c, 5, 0))
        up3 = jnp.where(row == 5, pltpu.roll(outer, 3, 0), up3)
        return jnp.where(odd_row, c - predicted(down1, up1, down3, up3), c)

    def coarse_y(c, outer):
        down2 = pltpu.roll(c, 2, 0)
        further = pltpu.roll(c, 6, 0)
        beyond = pltpu.roll(outer, 2, 0)
        up2 = jnp.where(row == 6, pltpu.roll(outer, 4, 0), further)
        down6 = jnp.where(row == 2, beyond, further)
        up6 = jnp.where(row == 2, outer, beyond)
        return jnp.where(mid_row, c - predicted(down2, up2, down6, up6), c)

    def lift_zy(x, out, along_z, along_y):
        cells, outer = after(x), after_around(x)
        for f in range(2):
            tips = pltpu.roll(fc[f, slot(0), :], (252 - 16 * x) % LZ, 1)
            tips_outer = pltpu.roll(fc[f, slot(1), :], (252 - 16 * x) % LZ, 1)
            out[f, slot(x), :] = along_y(along_z(cells[f], tips), along_z(outer[f], tips_outer))

    def lift_fine(x):
        lift_zy(x, fn, fine_z, fine_y)

    def lift_coarse(x):
        lift_zy(x, fy, coarse_z, coarse_y)

    to_high = remote(sx_hi, rx_lo, lift_send.at[16], lift_recv.at[16], at(dx=1))
    to_low = remote(sx_lo, rx_hi, lift_send.at[17], lift_recv.at[17], at(dx=-1))
    lift_fine(6)
    lift_coarse(4)
    for f in range(2):
        sx_hi[f, slot(0), :] = fn[f, slot(6), :]
        sx_hi[f, slot(1), :] = fy[f, slot(4), :]
    to_high.start()
    lift_fine(0)
    lift_fine(2)
    lift_coarse(0)
    for f in range(2):
        sx_lo[f, slot(0), :] = fn[f, slot(0), :]
        sx_lo[f, slot(1), :] = fn[f, slot(2), :]
        sx_lo[f, slot(2), :] = jnp.where(odd_row, pltpu.roll(fy[f, slot(4), :], 1, 0), fy[f, slot(0), :])
    to_low.start()

    def update(x, _):
        for k in range(NF):
            r = SECTION_DECAY * rg[k, x] + step * plane(1, k, x)
            rn[k, x] = r
            sn[k, x] = st[k, x] + SECTION_GAIN * r
        return 0

    lax.fori_loop(0, LX, update, 0, unroll=4)
    store_state = pltpu.make_async_copy(sn, o_state, local_sem.at[2])
    store_reg = pltpu.make_async_copy(rn, o_reg, local_sem.at[3])
    store_state.start()
    store_reg.start()

    for x in (4, 1, 3, 5, 7):
        lift_fine(x)
    for x in (2, 6):
        lift_coarse(x)
    for copy in halos + lifts[0] + lifts[1]:
        copy.wait_send()
    for i in range(3):
        max_sent(i)

    to_high.wait_recv()
    to_low.wait_recv()
    even = jnp.logical_and(row % 2 == 0, lane % 2 == 0)
    for f in range(2):
        fine = {x: fn[f, slot(x), :] for x in range(LX)}
        fine[-2], fine[8], fine[10] = rx_lo[f, slot(0), :], rx_hi[f, slot(0), :], rx_hi[f, slot(1), :]
        coarse = {x: fy[f, slot(x), :] for x in (0, 2, 4, 6)}
        mixed = rx_hi[f, slot(2), :]
        coarse[-4], coarse[8], coarse[12] = rx_lo[f, slot(1), :], mixed, pltpu.roll(mixed, 7, 0)
        for x in range(LX):
            if x % 2 == 1:
                coef[f, x] = fine[x] - predicted(fine[x - 1], fine[x + 1], fine[x - 3], fine[x + 3])
                continue
            value = coarse[x]
            if x % 4 == 2:
                value = value - predicted(coarse[x - 2], coarse[x + 2], coarse[x - 6], coarse[x + 6])
            coef[f, x] = jnp.where(even, value, fine[x])
    store_coef = pltpu.make_async_copy(coef, o_coef, local_sem.at[4])
    store_coef.start()

    to_high.wait_send()
    to_low.wait_send()
    store_state.wait()
    store_reg.wait()
    store_coef.wait()


def deliver(*refs):
    sources, targets, stages, sems = refs[:3], refs[3:6], refs[6:9], refs[9]
    loads = [pltpu.make_async_copy(sources[i], stages[i], sems.at[i]) for i in range(3)]
    stores = [pltpu.make_async_copy(stages[i], targets[i], sems.at[3 + i]) for i in range(3)]
    for load in loads:
        load.start()
    for load, store in zip(loads, stores):
        load.wait()
        store.start()
    for store in stores:
        store.wait()


def solution(mesh):
    sizes = (mesh.shape["gx"], mesh.shape["gy"], mesh.shape["gz"])
    spec = P(None, "gx", "gy", "gz")
    any_space = pl.BlockSpec(memory_space=pl.ANY)

    def vmem(*shape):
        return pltpu.VMEM(shape, F32)

    plane = (8, LZ)
    total = sizes[0] // 2 + sizes[1] + 2 * sizes[2]
    scratch = [
        vmem(NF, LX, *plane),
        vmem(NF, LX, *plane),
        vmem(NF, SPARE + 8, LZ),
        vmem(NF, SPARE, LZ),
        vmem(NF, *plane),
        vmem(NF, *plane),
        vmem(NF, *plane),
        vmem(2, NF, (LX + 2) * 8, LZ),
        vmem(2, NF, (LX + 2) * 8, LZ),
        vmem(NF, (LX + 1) * 8, LZ),
        vmem(NF, (LX + 2) * 8, LZ),
        vmem(NF, (LX + 1) * 8, LZ),
        vmem(NF, LX, *plane),
        vmem(NF, LX, *plane),
        vmem(NF, (LX + 1) * 8, LZ),
        vmem(NF, (LX + 1) * 8, LZ),
        vmem(2, NF, 16, LZ),
        vmem(2, NF, 40, LZ),
        vmem(2, NF, 72, LZ),
        vmem(2, 16, LZ),
        vmem(2, 24, LZ),
        vmem(2, 16, LZ),
        vmem(2, 24, LZ),
        vmem(2, NF, *plane),
        vmem(2, 6, NF, *plane),
        vmem(2, 64, LZ),
        vmem(2, 64, LZ),
        vmem(2, 16, LZ),
        vmem(2, LX, *plane),
        vmem(sizes[0] // 2, 1, LZ),
        vmem(sizes[1], 1, LZ),
        vmem(2 * sizes[2], 1, LZ),
        pltpu.SemaphoreType.DMA((5,)),
        pltpu.SemaphoreType.DMA((6,)),
        pltpu.SemaphoreType.DMA((6,)),
        pltpu.SemaphoreType.DMA((total,)),
        pltpu.SemaphoreType.DMA((total,)),
        pltpu.SemaphoreType.DMA((18,)),
        pltpu.SemaphoreType.DMA((18,)),
        pltpu.SemaphoreType.REGULAR((3,)),
    ]

    def local(state, register):
        block = jax.ShapeDtypeStruct(state.shape, F32)
        shapes = (block, block, jax.ShapeDtypeStruct((2,) + state.shape[1:], F32))
        results = pl.pallas_call(
            functools.partial(kernel, sizes),
            out_shape=shapes,
            in_specs=[any_space] * 2,
            out_specs=(any_space,) * 3,
            scratch_shapes=scratch,
            compiler_params=pltpu.CompilerParams(collective_id=0, has_side_effects=True),
        )(state, register)
        return pl.pallas_call(
            deliver,
            out_shape=shapes,
            in_specs=[any_space] * 3,
            out_specs=(any_space,) * 3,
            scratch_shapes=[pltpu.VMEM(shape.shape, F32) for shape in shapes] + [pltpu.SemaphoreType.DMA((6,))],
        )(*results)

    return jax.shard_map(local, mesh=mesh, in_specs=(spec, spec), out_specs=(spec,) * 3, check_vma=False)
```
